32 devices in a mesh: tm: 8 (over z, x), batch: 4 (over y, core).
Axes of the slice: x: 2, y: 2, z: 4, core: 2. Of those that a mesh axis runs over, the one named last changes fastest.
Arguments:
- state: float32 [8, 4, 256, 1152], P('tm', 'batch'), may hold values from -6 to 6
- noise_draws: bfloat16 [2, 8, 4, 256, 1152], P(None, 'tm', 'batch'), may hold values from -6 to 6
- class_vec: float32 [4, 1152], P('batch'), may hold values from -6 to 6
- window_start: int32 [4], P('batch'), may hold values from 0 to 985
- advance: int32 [4], P('batch'), may hold values from 1 to 7
- step_dt: float32 [1000], replicated, may hold values from 0.05 to 0.2
- step_sigma: float32 [1000], replicated, may hold values from 0.05 to 0.2
- w_ada: bfloat16 [1152, 3456], replicated, may hold values from -0.1875 to 0.1875
- w_up: bfloat16 [4608, 1152], P(('tm', 'batch')), may hold values from -0.1875 to 0.1875
- w_down: bfloat16 [4608, 1152], P(('tm', 'batch')), may hold values from -0.09375 to 0.09375
Outputs:
- window_out: float32 [8, 4, 256, 1152], P('tm', 'batch')
The draws below stay inside these ranges and needn't reach their ends.
All inputs are finite; a program needn't handle non-finite values.
Results may differ from the reference program's by a relative error of at most 0.0037.
Values may be sent and summed in bfloat16 or wider, within the bound.
A program may use at most 128 MiB of HBM per device.

```python
import math
import jax
import jax.numpy as jnp
from jax import lax

D = 1152
LAT = 256
FF = 4608
TRAJ = 1000
SWEEPS = 2
ADV_MAX = 7
WINDOW = 8
IMAGES = 4


def plant(values, rng, low, largest):
    longest = values.shape.index(max(values.shape))
    spots = []
    for shift in (0, 1):
        where = [jax.random.randint(jax.random.fold_in(rng, axis), (), 0, length) for axis, length in enumerate(values.shape)]
        where[longest] = (where[longest] + shift) % values.shape[longest]
        spots.append(tuple(where))
    return values.at[spots[0]].set(low).at[spots[1]].set(largest)


def steps_of(own_key, dims, shards, least, top_value):
    def one(position, shards_of):
        steps = jax.random.uniform(jax.random.fold_in(jax.random.fold_in(own_key, 6), position), (shards_of,), jnp.float32, least / len(shards), top_value / len(shards))
        return jnp.repeat(jnp.exp(steps), dims[position] // shards_of).reshape((-1,) + (1,) * (len(dims) - position - 1))

    loudness = one(*shards[0])
    for cut in shards[1:]:
        loudness = loudness * one(*cut)
    return loudness


def noise(rng, shape, deviation, limit, cuts=(), kind=jnp.bfloat16):
    factor_of = steps_of(rng, shape, cuts, -0.22, 0.18) if cuts else 1.0
    entries = jax.random.normal(rng, shape, jnp.float32) * deviation * factor_of
    return jnp.minimum(jnp.maximum(entries, -limit), limit).astype(kind)


def setup_inputs(seed: int = 0) -> dict:
    keys = jax.random.split(jax.random.key(seed), 11)
    state = noise(keys[0], (WINDOW, IMAGES, LAT, D), 1.0, 6.0, ((0, 8), (1, 4)), jnp.float32)
    noise_draws = noise(keys[1], (SWEEPS, WINDOW, IMAGES, LAT, D), 1.0, 6.0, ((1, 8), (2, 4)))
    class_vec = noise(keys[2], (IMAGES, D), 1.0, 6.0, ((0, 4),), jnp.float32)
    window_start = plant(jax.random.randint(keys[3], (IMAGES,), 0, TRAJ - WINDOW - ADV_MAX + 1), jax.random.fold_in(keys[3], 1), 0, TRAJ - WINDOW - ADV_MAX).astype(jnp.int32)
    advance = plant(jax.random.randint(keys[4], (IMAGES,), 1, ADV_MAX + 1), jax.random.fold_in(keys[4], 1), 1, ADV_MAX).astype(jnp.int32)
    step_dt = jnp.clip(jnp.exp(jax.random.uniform(keys[5], (TRAJ,), jnp.float32, math.log(0.05), math.log(0.2))), 0.05, 0.2)
    step_sigma = jnp.clip(jnp.exp(jax.random.uniform(keys[6], (TRAJ,), jnp.float32, math.log(0.05), math.log(0.2))), 0.05, 0.2)
    w_ada = noise(keys[7], (D, 3 * D), D ** -0.5, 0.1875)
    w_up = noise(keys[8], (FF, D), D ** -0.5, 0.1875, ((0, 32),))
    w_down = noise(keys[9], (FF, D), FF ** -0.5, 0.09375, ((0, 32),))
    return dict(state=state, noise_draws=noise_draws, class_vec=class_vec, window_start=window_start, advance=advance, step_dt=step_dt, step_sigma=step_sigma, w_ada=w_ada, w_up=w_up, w_down=w_down)


EPSILON = 1e-06

def time_embed(steps_now, half_width):
    frequency = jnp.exp(-math.log(10000.0) * jnp.arange(half_width, dtype=jnp.float32) / half_width)
    angles = steps_now.astype(jnp.float32)[:, None] * frequency[None, :]
    return jnp.concatenate([jnp.cos(angles), jnp.sin(angles)], axis=1)

def dense_pair(hidden_rows, up_rows, down_rows):
    before = lax.dot_general(hidden_rows, up_rows, (((1,), (1,)), ((), ())), preferred_element_type=jnp.float32)
    activated = jax.nn.gelu(before, approximate=True).astype(jnp.bfloat16)
    return jnp.dot(activated, down_rows, preferred_element_type=jnp.float32)

def increment(current, noise_now, steps_now, class_vec, step_dt, step_sigma, w_ada, w_up, w_down):
    images, tokens, channels = current.shape
    step_table = lax.iota(jnp.int32, step_dt.shape[0])
    onehot = (steps_now[:, None] == step_table[None, :]).astype(jnp.float32)
    step_size = lax.optimization_barrier(jnp.sum(onehot * step_dt[None, :], axis=1))
    spread = lax.optimization_barrier(jnp.sum(onehot * step_sigma[None, :], axis=1))
    condition = jax.nn.silu(time_embed(steps_now, channels // 2) + class_vec).astype(jnp.bfloat16)
    modulation = jnp.dot(condition, w_ada, preferred_element_type=jnp.float32)
    shift_by = modulation[:, :channels]
    scale_by = modulation[:, channels:2 * channels]
    gate_by = modulation[:, 2 * channels:]
    mean_val = lax.optimization_barrier(jnp.mean(current, axis=2, keepdims=True))
    centred = current - mean_val
    var_val = lax.optimization_barrier(jnp.mean(centred * centred, axis=2, keepdims=True))
    normed = centred * lax.rsqrt(var_val + EPSILON)
    hidden_in = (normed * (1.0 + scale_by[:, None, :]) + shift_by[:, None, :]).astype(jnp.bfloat16)
    mlp_out = dense_pair(hidden_in.reshape(images * tokens, channels), w_up, w_down).reshape(images, tokens, channels)
    drift = gate_by[:, None, :] * mlp_out - current
    return step_size[:, None, None] * drift + spread[:, None, None] * noise_now.astype(jnp.float32)

def pick_rows(column, source_index):
    return column[source_index]

def reference(state, noise_draws, class_vec, window_start, advance, step_dt, step_sigma, w_ada, w_up, w_down):
    window_size = state.shape[0]

    def sweep(states, noise_now, starts):

        def one_step(items):
            current, noise_step, offset = items
            return increment(current, noise_step, starts + offset, class_vec, step_dt, step_sigma, w_ada, w_up, w_down)
        increments = lax.map(one_step, (states, noise_now, jnp.arange(window_size, dtype=jnp.int32)))
        totals = jnp.cumsum(increments, axis=0)
        exclusive = jnp.concatenate([jnp.zeros_like(increments[:1]), totals[:-1]], axis=0)
        updated = states[0][None] + exclusive
        end_rows = states[0] + totals[-1]
        return (updated, end_rows)
    updated, end_rows = sweep(state, noise_draws[0], window_start)
    extended = jnp.concatenate([updated, end_rows[None]], axis=0)
    source_index = jnp.minimum(jnp.arange(window_size, dtype=jnp.int32)[:, None] + advance[None, :], window_size)
    slid = jax.vmap(pick_rows, in_axes=(1, 1), out_axes=1)(extended, source_index)
    final_rows, leftover = sweep(slid, noise_draws[1], window_start + advance)
    return final_rows
```

```python
import functools
import math

import jax
import jax.numpy as jnp
from jax import lax
from jax.experimental import pallas as pl
from jax.experimental.pallas import tpu as pltpu
from jax.sharding import PartitionSpec as P

SLIDE_BITS = 3
MESH = pl.DeviceIdType.MESH
WIN = 8
LAYERS = 4

EPSILON = 1e-06


def spread_2(shard, axis, root):
    mine = lax.axis_index(axis) == root
    return lax.psum(jnp.where(mine, shard, jnp.zeros_like(shard)), axis)


def carried_in(part, axis, combine, identity):
    place = lax.axis_index(axis)
    gathered = lax.all_gather(part, axis)
    state = jnp.zeros_like(part) + jnp.asarray(identity, part.dtype)

    def one(turn, state):
        return combine(state, lax.dynamic_index_in_dim(gathered, turn, 0, False))

    return lax.fori_loop(0, place, one, state)


def from_behind(shard, axis, by):
    peers = lax.axis_size(axis)
    pairs = [(i, i + by) for i in range(peers) if 0 <= i + by < peers]
    return lax.ppermute(shard, axis, pairs)


def time_embed(steps_now, half_width):
    frequency = jnp.exp(-math.log(10000.0) * jnp.arange(half_width, dtype=jnp.float32) / half_width)
    angles = steps_now.astype(jnp.float32)[:, None] * frequency[None, :]
    return jnp.concatenate([jnp.cos(angles), jnp.sin(angles)], axis=1)


def dense_pair(hidden_rows, up_rows, down_rows):
    before = lax.dot_general(
        hidden_rows, up_rows, (((1,), (1,)), ((), ())), preferred_element_type=jnp.float32
    )
    activated = jax.nn.gelu(before, approximate=True).astype(jnp.bfloat16)
    return jnp.dot(activated, down_rows, preferred_element_type=jnp.float32)


def combine_sum(earlier, later):
    return earlier + later


def increment(current, noise_now, steps_now, class_vec, step_dt, step_sigma, w_ada, mlp_apply):
    images, tokens, channels = current.shape
    step_table = lax.iota(jnp.int32, step_dt.shape[0])
    onehot = (steps_now[:, None] == step_table[None, :]).astype(jnp.float32)
    step_size = jnp.sum(onehot * step_dt[None, :], axis=1)
    spread = jnp.sum(onehot * step_sigma[None, :], axis=1)
    condition = jax.nn.silu(time_embed(steps_now, channels // 2) + class_vec).astype(jnp.bfloat16)
    modulation = jnp.dot(condition, w_ada, preferred_element_type=jnp.float32)
    shift_by = modulation[:, :channels]
    scale_by = modulation[:, channels : 2 * channels]
    gate_by = modulation[:, 2 * channels :]
    mean_val = jnp.mean(current, axis=2, keepdims=True)
    centred = current - mean_val
    var_val = jnp.mean(centred * centred, axis=2, keepdims=True)
    normed = centred * lax.rsqrt(var_val + EPSILON)
    hidden_in = (normed * (1.0 + scale_by[:, None, :]) + shift_by[:, None, :]).astype(jnp.bfloat16)
    mlp_out = mlp_apply(hidden_in.reshape(images * tokens, channels)).reshape(
        images, tokens, channels
    )
    drift = gate_by[:, None, :] * mlp_out - current
    return step_size[:, None, None] * drift + spread[:, None, None] * noise_now.astype(jnp.float32)


def per_device(
    state, noise_draws, class_vec, window_start, advance, step_dt, step_sigma, w_ada, w_up, w_down
):
    window_size = lax.axis_size("tm")
    position = lax.axis_index("tm")
    up_whole, down_whole = (
        lax.all_gather(w_up, ("tm", "batch"), axis=0, tiled=True),
        lax.all_gather(w_down, ("tm", "batch"), axis=0, tiled=True),
    )

    def mlp_apply(hidden_rows):
        return dense_pair(hidden_rows, up_whole, down_whole)

    def sweep(current, noise_now, starts):
        steps_now = starts + position
        step_inc = increment(
            current, noise_now, steps_now, class_vec, step_dt, step_sigma, w_ada, mlp_apply
        )
        base_rows = spread_2(current, "tm", 0)
        prefix = carried_in(step_inc, "tm", combine_sum, jnp.zeros_like(step_inc))
        updated = base_rows + prefix
        return (updated, step_inc)

    updated, step_inc = sweep(state[0], noise_draws[0, 0], window_start)
    end_rows = updated + step_inc
    tail_rows = jnp.where(position == window_size - 1, end_rows, jnp.zeros_like(end_rows))
    moved = updated
    for section_bit in range(SLIDE_BITS):
        distance = 1 << section_bit
        arrived, arrived_tail = from_behind((moved, tail_rows), "tm", -distance)
        taken = advance >> section_bit & 1 == 1
        outside = position + distance >= window_size
        incoming = jnp.where(outside, tail_rows, arrived)
        moved = jnp.where(taken[:, None, None], incoming, moved)
        tail_rows = jnp.where(position >= window_size - distance, tail_rows, arrived_tail)
    final_rows, leftover = sweep(moved, noise_draws[1, 0], window_start + advance)
    return final_rows[None]


def fused(
    start_ref, adv_ref, dt_ref, sg_ref, cls_ref, state_ref, noise_ref, wup_ref, wdn_ref, wada_ref,
    out_ref,
    up_full, dn_full, ada_buf, mod, a_send, a_recv, lo_send, lo_recv, cur, hid, acc, pre, o_send,
    loc_sem, w_recv, z_sem, x_sem, y_sem, s_sem, a_ssem, a_rsem, l_ssem, l_rsem, o_ssem, o_rsem,
):
    tokens, width = state_ref.shape
    part = tokens // WIN
    depth = wup_ref.shape[0]
    layer = 8 * depth
    tm, bt = lax.axis_index("tm"), lax.axis_index("batch")
    z, x = tm // 2, tm % 2
    y, c = bt // 2, bt % 2
    xn, yn, cn = 1 - x, 1 - y, 1 - c

    def dev(zz, xx, yy, cc):
        return (zz * 2 + xx, yy * 2 + cc)

    x_dev, y_dev, s_dev = dev(z, xn, y, c), dev(z, x, yn, c), dev(z, x, y, cn)
    up_dev, down_dev = dev(z + 1, x, y, c), dev(z - 1, x, y, c)

    barrier = pltpu.get_barrier_semaphore()
    for d in range(1, WIN):
        pl.semaphore_signal(barrier, inc=1, device_id=((tm + d) % WIN, bt), device_id_type=MESH)
    pl.semaphore_signal(barrier, inc=1, device_id=y_dev, device_id_type=MESH)
    pl.semaphore_signal(barrier, inc=1, device_id=s_dev, device_id_type=MESH)
    pl.semaphore_wait(barrier, WIN + 1)

    full = (up_full, dn_full)
    given = (wup_ref, wdn_ref)

    def block(w, sid):
        return full[w].at[pl.ds(pl.multiple_of(sid * depth, 16), depth)]

    def ident(zz, xx, yy, cc):
        return (zz * 2 + xx) * 4 + yy * 2 + cc

    def send(w, sid, to, sem, own=False):
        pltpu.make_async_remote_copy(
            src_ref=given[w] if own else block(w, sid), dst_ref=block(w, sid),
            send_sem=sem, recv_sem=w_recv.at[w, sid], device_id=to, device_id_type=MESH,
        ).start()

    def arrive(w, sid):
        pltpu.make_async_remote_copy(
            src_ref=block(w, sid), dst_ref=block(w, sid),
            send_sem=s_sem.at[w, 0, 0], recv_sem=w_recv.at[w, sid], device_id=s_dev, device_id_type=MESH,
        ).wait_recv()

    def sent(w, sem):
        pltpu.make_async_remote_copy(
            src_ref=given[w], dst_ref=block(w, 0),
            send_sem=sem, recv_sem=w_recv.at[w, 0], device_id=s_dev, device_id_type=MESH,
        ).wait_send()

    def spread(zz, own=False):
        sid = ident(zz, x, y, c)
        for w in (0, 1):
            send(w, sid, x_dev, x_sem.at[w, 0, zz], own)
            send(w, sid, y_dev, y_sem.at[w, 0, zz], own)
        for w in (0, 1):
            send(w, sid, s_dev, s_sem.at[w, 0, zz], own)

    def side(zz):
        from_x, from_y = ident(zz, xn, y, c), ident(zz, x, yn, c)
        arrive(0, from_x)
        send(0, from_x, y_dev, y_sem.at[0, 1, zz])
        arrive(1, from_y)
        send(1, from_y, x_dev, x_sem.at[1, 1, zz])
        arrive(1, from_x)
        arrive(0, from_y)
        for w in (0, 1):
            send(w, from_x, s_dev, s_sem.at[w, 1, zz])
            send(w, from_y, s_dev, s_sem.at[w, 2, zz])

    me = ident(z, x, y, c)

    @pl.when(z < LAYERS - 1)
    def _():
        for w in (0, 1):
            send(w, me, up_dev, z_sem.at[w, 0, z], True)

    @pl.when(z > 0)
    def _():
        for w in (0, 1):
            send(w, me, down_dev, z_sem.at[w, 1, z], True)

    spread(z, True)
    local = [
        pltpu.make_async_copy(wada_ref, ada_buf, loc_sem.at[0]),
        pltpu.make_async_copy(wup_ref, block(0, me), loc_sem.at[1]),
        pltpu.make_async_copy(wdn_ref, block(1, me), loc_sem.at[2]),
    ]
    for copy in local:
        copy.start()

    for t in range(WIN):
        rows = pl.ds(t * part, part)
        whole = state_ref[rows, :]
        high = whole.astype(jnp.bfloat16)
        a_send[t, 0:part, :] = high
        lo_send[t] = (whole - high.astype(jnp.float32)).astype(jnp.bfloat16)
        a_send[t, part : 2 * part, :] = noise_ref[0, rows, :]
        a_send[t, 2 * part : 3 * part, :] = noise_ref[1, rows, :]
    a_recv[tm] = a_send[tm]

    start, adv = start_ref[0], adv_ref[0]
    row = lax.broadcasted_iota(jnp.int32, (2 * WIN, width), 0)
    lane = lax.broadcasted_iota(jnp.int32, (2 * WIN, width), 1)
    half = width // 2
    late = row >= WIN
    steps = (start + jnp.where(late, adv + row - WIN, row)).astype(jnp.float32)
    turn = jnp.where(lane >= half, lane - half, lane).astype(jnp.float32)
    angles = steps * jnp.exp(-math.log(10000.0) * turn / half)
    embed = jnp.where(lane >= half, jnp.sin(angles), jnp.cos(angles))
    condition = jax.nn.silu(embed + cls_ref[...]).astype(jnp.bfloat16)
    for copy in local:
        copy.wait()
    for third in range(3):
        columns = slice(third * width, (third + 1) * width)
        mod[:, columns] = jnp.dot(condition, ada_buf[:, columns], preferred_element_type=jnp.float32)

    def a_copy(d):
        to = (tm + d) % WIN
        return pltpu.make_async_remote_copy(
            src_ref=a_send.at[to], dst_ref=a_recv.at[tm], send_sem=a_ssem.at[d],
            recv_sem=a_rsem.at[tm], device_id=(to, bt), device_id_type=MESH,
        )

    def l_copy(d):
        return pltpu.make_async_remote_copy(
            src_ref=lo_send.at[d], dst_ref=lo_recv, send_sem=l_ssem.at[d],
            recv_sem=l_rsem, device_id=(d, bt), device_id_type=MESH,
        )

    def round_z(r):
        @pl.when(z >= r)
        def _():
            zz = z - r
            sid = ident(zz, x, y, c)
            for w in (0, 1):
                arrive(w, sid)

                @pl.when(z < LAYERS - 1)
                def _():
                    send(w, sid, up_dev, z_sem.at[w, 0, zz])

            spread(zz)

        @pl.when(z + r < LAYERS)
        def _():
            zz = z + r
            sid = ident(zz, x, y, c)
            for w in (0, 1):
                arrive(w, sid)

                @pl.when(z > 0)
                def _():
                    send(w, sid, down_dev, z_sem.at[w, 1, zz])

            spread(zz)

    def round_side(r):
        if r == 0:
            side(z)
            return

        @pl.when(z >= r)
        def _():
            side(z - r)

        @pl.when(z + r < LAYERS)
        def _():
            side(z + r)

    round_z(1)
    round_side(0)
    round_z(2)
    for d in range(1, WIN):
        a_copy(d).start()

    @pl.when(tm == 0)
    def _():
        lo_recv[...] = lo_send[0]
        for d in range(1, WIN):
            l_copy(d).start()

    round_side(1)
    round_z(3)
    round_side(2)
    round_side(3)

    def a_arrive(d):
        src = (tm + d) % WIN
        pltpu.make_async_remote_copy(
            src_ref=a_send.at[src], dst_ref=a_recv.at[src], send_sem=a_ssem.at[d],
            recv_sem=a_rsem.at[src], device_id=(src, bt), device_id_type=MESH,
        ).wait_recv()

    for d in range(1, WIN):
        a_arrive(d)

    @pl.when(tm > 0)
    def _():
        l_copy(1).wait_recv()

    for j in range(WIN):
        cur[j] = a_recv[j, 0:part, :].astype(jnp.float32)

    def before_mlp(s):
        @pl.loop(0, WIN)
        def _(j):
            now = cur[j]
            centred = now - jnp.mean(now, axis=1, keepdims=True)
            var = jnp.mean(centred * centred, axis=1, keepdims=True)
            normed = centred * lax.rsqrt(var + EPSILON)
            shift = mod[pl.ds(s * WIN + j, 1), 0:width]
            scale = mod[pl.ds(s * WIN + j, 1), width : 2 * width]
            rows = pl.ds(pl.multiple_of(j * part, part), part)
            hid[rows, :] = (normed * (1.0 + scale) + shift).astype(jnp.bfloat16)
            acc[rows, :] = jnp.zeros((part, width), jnp.float32)

    def mlp(first, count):
        rows = pl.ds(pl.multiple_of(first, 128), count)
        before = lax.dot_general(
            hid[...], up_full[rows, :], (((1,), (1,)), ((), ())), preferred_element_type=jnp.float32
        )
        act = jax.nn.gelu(before, approximate=True).astype(jnp.bfloat16)
        acc[...] += jnp.dot(act, dn_full[rows, :], preferred_element_type=jnp.float32)

    def after_mlp(s, base):
        pre[0] = base
        for j in range(WIN):
            k = start + s * adv + j
            rows = pl.ds(j * part, part)
            gate = mod[s * WIN + j : s * WIN + j + 1, 2 * width : 3 * width]
            noise = a_recv[j, (1 + s) * part : (2 + s) * part, :].astype(jnp.float32)
            pre[j + 1] = pre[j] + (dt_ref[k] * (gate * acc[rows, :] - cur[j]) + sg_ref[k] * noise)

    before_mlp(0)
    flip = z // 2
    near = z + flip * (3 - 2 * z)

    @pl.loop(0, LAYERS)
    def _(p):
        early = 1 - p // 2
        order = p + near * early * (1 - 2 * p)
        zz = order + flip * (3 - 2 * order)
        across = ident(zz, xn, yn, c)
        for w in (0, 1):
            arrive(w, across)
            send(w, across, s_dev, s_sem.at[w, 3, zz])
        for xx in (0, 1):
            for yy in (0, 1):
                for w in (0, 1):
                    arrive(w, ident(zz, xx, yy, cn))

        @pl.loop(0, 3)
        def _(i):
            mlp(zz * layer + i * (layer // 3), layer // 3)

    after_mlp(0, cur[0] + lo_recv[...].astype(jnp.float32))
    for j in range(WIN):
        cur[j] = pre[jnp.minimum(adv + j, WIN)]
    before_mlp(1)

    @pl.loop(0, 3)
    def _(i):
        for k in range(3):
            mlp((i * 3 + k) * (LAYERS * layer // 9), LAYERS * layer // 9)

    after_mlp(1, cur[0])
    for j in range(WIN):
        o_send[j] = pre[j].astype(jnp.bfloat16)

    own_rows = pl.ds(pl.multiple_of(tm * part, part), part)

    def o_copy(d):
        to = (tm + d) % WIN
        return pltpu.make_async_remote_copy(
            src_ref=o_send.at[to], dst_ref=out_ref.at[own_rows], send_sem=o_ssem.at[d],
            recv_sem=o_rsem.at[tm], device_id=(to, bt), device_id_type=MESH,
        )

    def o_arrive(d):
        src = (tm + d) % WIN
        pltpu.make_async_remote_copy(
            src_ref=o_send.at[src],
            dst_ref=out_ref.at[pl.ds(pl.multiple_of(src * part, part), part)],
            send_sem=o_ssem.at[d], recv_sem=o_rsem.at[src], device_id=(src, bt), device_id_type=MESH,
        ).wait_recv()

    for d in range(1, WIN):
        o_copy(d).start()
    mine = pltpu.make_async_copy(o_send.at[tm], out_ref.at[own_rows], loc_sem.at[0])
    mine.start()

    for zz in range(LAYERS):
        for w in (0, 1):
            @pl.when((z < LAYERS - 1) & (zz <= z))
            def _():
                sent(w, z_sem.at[w, 0, zz])

            @pl.when((z > 0) & (zz >= z))
            def _():
                sent(w, z_sem.at[w, 1, zz])

            sent(w, x_sem.at[w, 0, zz])
            sent(w, y_sem.at[w, 0, zz])
            for kind in range(4):
                sent(w, s_sem.at[w, kind, zz])
        sent(0, y_sem.at[0, 1, zz])
        sent(1, x_sem.at[1, 1, zz])
    for d in range(1, WIN):
        a_copy(d).wait_send()

    @pl.when(tm == 0)
    def _():
        for d in range(1, WIN):
            l_copy(d).wait_send()

    mine.wait()
    for d in range(1, WIN):
        o_arrive(d)
        o_copy(d).wait_send()


def per_device_fused(
    state, noise_draws, class_vec, window_start, advance, step_dt, step_sigma, w_ada, w_up, w_down
):
    tokens, width = state.shape[2:]
    hidden = w_up.shape[0] * WIN * 4
    part = tokens // WIN
    bf16, f32 = jnp.bfloat16, jnp.float32
    vmem, smem = pl.BlockSpec(memory_space=pltpu.VMEM), pl.BlockSpec(memory_space=pltpu.SMEM)
    dma = pltpu.SemaphoreType.DMA
    flops = 2 * 2 * 2 * tokens * width * hidden
    out = pl.pallas_call(
        fused,
        out_shape=jax.ShapeDtypeStruct((tokens, width), bf16),
        in_specs=[smem] * 4 + [vmem] * 5 + [pl.BlockSpec(memory_space=pl.ANY)],
        out_specs=pl.BlockSpec(memory_space=pl.ANY),
        scratch_shapes=[
            pltpu.VMEM((hidden, width), bf16),
            pltpu.VMEM((hidden, width), bf16),
            pltpu.VMEM(w_ada.shape, bf16),
            pltpu.VMEM((2 * WIN, 3 * width), f32),
            pltpu.VMEM((WIN, 3 * part, width), bf16),
            pltpu.VMEM((WIN, 3 * part, width), bf16),
            pltpu.VMEM((WIN, part, width), bf16),
            pltpu.VMEM((part, width), bf16),
            pltpu.VMEM((WIN, part, width), f32),
            pltpu.VMEM((tokens, width), bf16),
            pltpu.VMEM((tokens, width), f32),
            pltpu.VMEM((WIN + 1, part, width), f32),
            pltpu.VMEM((WIN, part, width), bf16),
            dma((3,)),
            dma((2, 32)),
            dma((2, 2, LAYERS)),
            dma((2, 2, LAYERS)),
            dma((2, 2, LAYERS)),
            dma((2, 4, LAYERS)),
            dma((WIN,)),
            dma((WIN,)),
            dma((WIN,)),
            dma,
            dma((WIN,)),
            dma((WIN,)),
        ],
        compiler_params=pltpu.CompilerParams(
            collective_id=0, has_side_effects=True, vmem_limit_bytes=58 * 2**20
        ),
        cost_estimate=pl.CostEstimate(flops=flops, bytes_accessed=2 * w_ada.size, transcendentals=0),
        name="picard",
    )(
        window_start, advance, step_dt, step_sigma, class_vec,
        state[0, 0], noise_draws[:, 0, 0], w_up, w_down, w_ada,
    )
    return out.astype(f32)[None, None]


def solution(mesh):
    in_specs = (
        P("tm", "batch", None, None),
        P(None, "tm", "batch", None, None),
        P("batch", None),
        P("batch"),
        P("batch"),
        P(),
        P(),
        P(),
        P(("tm", "batch"), None),
        P(("tm", "batch"), None),
    )
    out_specs = P("tm", "batch", None, None)
    small = mesh.shape["tm"] == WIN and mesh.shape["batch"] == 4
    return jax.shard_map(
        per_device_fused if small else per_device,
        mesh=mesh, in_specs=in_specs, out_specs=out_specs, check_vma=False,
    )
```

```python
import functools
import math

import jax
import jax.numpy as jnp
from jax import lax
from jax.experimental import pallas as pl
from jax.experimental.pallas import tpu as pltpu
from jax.sharding import PartitionSpec as P

SLIDE_BITS = 3
MESH = pl.DeviceIdType.MESH
WIN = 8
LAYERS = 4

EPSILON = 1e-06


def spread_2(shard, axis, root):
    mine = lax.axis_index(axis) == root
    return lax.psum(jnp.where(mine, shard, jnp.zeros_like(shard)), axis)


def carried_in(part, axis, combine, identity):
    place = lax.axis_index(axis)
    gathered = lax.all_gather(part, axis)
    state = jnp.zeros_like(part) + jnp.asarray(identity, part.dtype)

    def one(turn, state):
        return combine(state, lax.dynamic_index_in_dim(gathered, turn, 0, False))

    return lax.fori_loop(0, place, one, state)


def from_behind(shard, axis, by):
    peers = lax.axis_size(axis)
    pairs = [(i, i + by) for i in range(peers) if 0 <= i + by < peers]
    return lax.ppermute(shard, axis, pairs)


def time_embed(steps_now, half_width):
    frequency = jnp.exp(-math.log(10000.0) * jnp.arange(half_width, dtype=jnp.float32) / half_width)
    angles = steps_now.astype(jnp.float32)[:, None] * frequency[None, :]
    return jnp.concatenate([jnp.cos(angles), jnp.sin(angles)], axis=1)


def dense_pair(hidden_rows, up_rows, down_rows):
    before = lax.dot_general(
        hidden_rows, up_rows, (((1,), (1,)), ((), ())), preferred_element_type=jnp.float32
    )
    activated = jax.nn.gelu(before, approximate=True).astype(jnp.bfloat16)
    return jnp.dot(activated, down_rows, preferred_element_type=jnp.float32)


def combine_sum(earlier, later):
    return earlier + later


def increment(current, noise_now, steps_now, class_vec, step_dt, step_sigma, w_ada, mlp_apply):
    images, tokens, channels = current.shape
    step_table = lax.iota(jnp.int32, step_dt.shape[0])
    onehot = (steps_now[:, None] == step_table[None, :]).astype(jnp.float32)
    step_size = jnp.sum(onehot * step_dt[None, :], axis=1)
    spread = jnp.sum(onehot * step_sigma[None, :], axis=1)
    condition = jax.nn.silu(time_embed(steps_now, channels // 2) + class_vec).astype(jnp.bfloat16)
    modulation = jnp.dot(condition, w_ada, preferred_element_type=jnp.float32)
    shift_by = modulation[:, :channels]
    scale_by = modulation[:, channels : 2 * channels]
    gate_by = modulation[:, 2 * channels :]
    mean_val = jnp.mean(current, axis=2, keepdims=True)
    centred = current - mean_val
    var_val = jnp.mean(centred * centred, axis=2, keepdims=True)
    normed = centred * lax.rsqrt(var_val + EPSILON)
    hidden_in = (normed * (1.0 + scale_by[:, None, :]) + shift_by[:, None, :]).astype(jnp.bfloat16)
    mlp_out = mlp_apply(hidden_in.reshape(images * tokens, channels)).reshape(
        images, tokens, channels
    )
    drift = gate_by[:, None, :] * mlp_out - current
    return step_size[:, None, None] * drift + spread[:, None, None] * noise_now.astype(jnp.float32)


def per_device(
    state, noise_draws, class_vec, window_start, advance, step_dt, step_sigma, w_ada, w_up, w_down
):
    window_size = lax.axis_size("tm")
    position = lax.axis_index("tm")
    up_whole, down_whole = (
        lax.all_gather(w_up, ("tm", "batch"), axis=0, tiled=True),
        lax.all_gather(w_down, ("tm", "batch"), axis=0, tiled=True),
    )

    def mlp_apply(hidden_rows):
        return dense_pair(hidden_rows, up_whole, down_whole)

    def sweep(current, noise_now, starts):
        steps_now = starts + position
        step_inc = increment(
            current, noise_now, steps_now, class_vec, step_dt, step_sigma, w_ada, mlp_apply
        )
        base_rows = spread_2(current, "tm", 0)
        prefix = carried_in(step_inc, "tm", combine_sum, jnp.zeros_like(step_inc))
        updated = base_rows + prefix
        return (updated, step_inc)

    updated, step_inc = sweep(state[0], noise_draws[0, 0], window_start)
    end_rows = updated + step_inc
    tail_rows = jnp.where(position == window_size - 1, end_rows, jnp.zeros_like(end_rows))
    moved = updated
    for section_bit in range(SLIDE_BITS):
        distance = 1 << section_bit
        arrived, arrived_tail = from_behind((moved, tail_rows), "tm", -distance)
        taken = advance >> section_bit & 1 == 1
        outside = position + distance >= window_size
        incoming = jnp.where(outside, tail_rows, arrived)
        moved = jnp.where(taken[:, None, None], incoming, moved)
        tail_rows = jnp.where(position >= window_size - distance, tail_rows, arrived_tail)
    final_rows, leftover = sweep(moved, noise_draws[1, 0], window_start + advance)
    return final_rows[None]


SPLIT = (0, 2, 6, 9)
TURNED = 2


def fused(
    start_ref, adv_ref, dt_ref, sg_ref, cls_ref, state_ref, noise_ref, wup_ref, wdn_ref, wada_ref,
    out_ref,
    up_full, dn_full, ada_buf, mod, a_send, a_recv, lo_send, lo_recv, cur, hid, acc, pre, o_send, act_all,
    loc_sem, w_recv, z_sem, x_sem, y_sem, s_sem, a_ssem, a_rsem, n_ssem, n_rsem, l_ssem, l_rsem, o_ssem, o_rsem,
):
    tokens, width = state_ref.shape
    part = tokens // WIN
    depth = wup_ref.shape[0]
    layer = 8 * depth
    tm, bt = lax.axis_index("tm"), lax.axis_index("batch")
    z, x = tm // 2, tm % 2
    y, c = bt // 2, bt % 2
    xn, yn, cn = 1 - x, 1 - y, 1 - c

    def dev(zz, xx, yy, cc):
        return (zz * 2 + xx, yy * 2 + cc)

    x_dev, y_dev, s_dev = dev(z, xn, y, c), dev(z, x, yn, c), dev(z, x, y, cn)
    up_dev, down_dev = dev(z + 1, x, y, c), dev(z - 1, x, y, c)

    barrier = pltpu.get_barrier_semaphore()
    for d in range(1, WIN):
        pl.semaphore_signal(barrier, inc=1, device_id=((tm + d) % WIN, bt), device_id_type=MESH)
    pl.semaphore_signal(barrier, inc=1, device_id=y_dev, device_id_type=MESH)
    pl.semaphore_signal(barrier, inc=1, device_id=s_dev, device_id_type=MESH)
    pl.semaphore_wait(barrier, WIN + 1)

    full = (up_full, dn_full)
    given = (wup_ref, wdn_ref)

    def block(w, sid):
        return full[w].at[pl.ds(pl.multiple_of(sid * depth, 16), depth)]

    def ident(zz, xx, yy, cc):
        return (zz * 2 + xx) * 4 + yy * 2 + cc

    def send(w, sid, to, sem, own=False):
        pltpu.make_async_remote_copy(
            src_ref=given[w] if own else block(w, sid), dst_ref=block(w, sid),
            send_sem=sem, recv_sem=w_recv.at[w, sid], device_id=to, device_id_type=MESH,
        ).start()

    def arrive(w, sid):
        pltpu.make_async_remote_copy(
            src_ref=block(w, sid), dst_ref=block(w, sid),
            send_sem=s_sem.at[w, 0, 0], recv_sem=w_recv.at[w, sid], device_id=s_dev, device_id_type=MESH,
        ).wait_recv()

    turned = depth * TURNED // 9 // 16 * 16
    cuts = ((0, turned), (turned, depth - turned))

    def piece(k, sid):
        return dn_full.at[pl.ds(pl.multiple_of(sid * depth + cuts[k][0], 16), cuts[k][1])]

    def piece_copy(k, sid, to, sem):
        return pltpu.make_async_remote_copy(
            src_ref=piece(k, sid), dst_ref=piece(k, sid),
            send_sem=sem, recv_sem=w_recv.at[1 + k, sid], device_id=to, device_id_type=MESH,
        )

    def sent(w, sem):
        pltpu.make_async_remote_copy(
            src_ref=given[w], dst_ref=block(w, 0),
            send_sem=sem, recv_sem=w_recv.at[w, 0], device_id=s_dev, device_id_type=MESH,
        ).wait_send()

    def spread(zz, own=False):
        sid = ident(zz, x, y, c)
        for w in (0, 1):
            send(w, sid, x_dev, x_sem.at[w, 0, zz], own)
            send(w, sid, y_dev, y_sem.at[w, 0, zz], own)
        for w in (0, 1):
            send(w, sid, s_dev, s_sem.at[w, 0, zz], own)

    def side(zz):
        from_x, from_y = ident(zz, xn, y, c), ident(zz, x, yn, c)
        arrive(0, from_x)
        send(0, from_x, y_dev, y_sem.at[0, 1, zz])
        arrive(1, from_y)
        piece_copy(1, from_y, x_dev, x_sem.at[1, 1, zz]).start()
        arrive(1, from_x)
        piece_copy(0, from_x, y_dev, y_sem.at[1, 1, zz]).start()
        arrive(0, from_y)
        for w in (0, 1):
            send(w, from_x, s_dev, s_sem.at[w, 1, zz])
            send(w, from_y, s_dev, s_sem.at[w, 2, zz])

    me = ident(z, x, y, c)

    @pl.when(z < LAYERS - 1)
    def _():
        for w in (0, 1):
            send(w, me, up_dev, z_sem.at[w, 0, z], True)

    @pl.when(z > 0)
    def _():
        for w in (0, 1):
            send(w, me, down_dev, z_sem.at[w, 1, z], True)

    spread(z, True)
    local = [
        pltpu.make_async_copy(wada_ref, ada_buf, loc_sem.at[0]),
        pltpu.make_async_copy(wup_ref, block(0, me), loc_sem.at[1]),
        pltpu.make_async_copy(wdn_ref, block(1, me), loc_sem.at[2]),
    ]
    for copy in local:
        copy.start()

    for t in range(WIN):
        rows = pl.ds(t * part, part)
        whole = state_ref[rows, :]
        high = whole.astype(jnp.bfloat16)
        a_send[t, 0:part, :] = high
        lo_send[t] = (whole - high.astype(jnp.float32)).astype(jnp.bfloat16)
        a_send[t, part : 2 * part, :] = noise_ref[0, rows, :]
        a_send[t, 2 * part : 3 * part, :] = noise_ref[1, rows, :]
    a_recv[tm] = a_send[tm]

    start, adv = start_ref[0], adv_ref[0]
    row = lax.broadcasted_iota(jnp.int32, (2 * WIN, width), 0)
    lane = lax.broadcasted_iota(jnp.int32, (2 * WIN, width), 1)
    half = width // 2
    late = row >= WIN
    steps = (start + jnp.where(late, adv + row - WIN, row)).astype(jnp.float32)
    turn = jnp.where(lane >= half, lane - half, lane).astype(jnp.float32)
    angles = steps * jnp.exp(-math.log(10000.0) * turn / half)
    embed = jnp.where(lane >= half, jnp.sin(angles), jnp.cos(angles))
    condition = jax.nn.silu(embed + cls_ref[...]).astype(jnp.bfloat16)
    for copy in local:
        copy.wait()
    for third in range(3):
        columns = slice(third * width, (third + 1) * width)
        mod[:, columns] = jnp.dot(condition, ada_buf[:, columns], preferred_element_type=jnp.float32)

    first, second = pl.ds(0, 2 * part), pl.ds(2 * part, part)

    def a_copy(d):
        to = (tm + d) % WIN
        return pltpu.make_async_remote_copy(
            src_ref=a_send.at[to, first], dst_ref=a_recv.at[tm, first], send_sem=a_ssem.at[d],
            recv_sem=a_rsem.at[tm], device_id=(to, bt), device_id_type=MESH,
        )

    def n_copy(d):
        to = (tm + d) % WIN
        return pltpu.make_async_remote_copy(
            src_ref=a_send.at[to, second], dst_ref=a_recv.at[tm, second], send_sem=n_ssem.at[d],
            recv_sem=n_rsem.at[tm], device_id=(to, bt), device_id_type=MESH,
        )

    def l_copy(d):
        return pltpu.make_async_remote_copy(
            src_ref=lo_send.at[d], dst_ref=lo_recv, send_sem=l_ssem.at[d],
            recv_sem=l_rsem, device_id=(d, bt), device_id_type=MESH,
        )

    def round_z(r):
        @pl.when(z >= r)
        def _():
            zz = z - r
            sid = ident(zz, x, y, c)
            for w in (0, 1):
                arrive(w, sid)

                @pl.when(z < LAYERS - 1)
                def _():
                    send(w, sid, up_dev, z_sem.at[w, 0, zz])

            spread(zz)

        @pl.when(z + r < LAYERS)
        def _():
            zz = z + r
            sid = ident(zz, x, y, c)
            for w in (0, 1):
                arrive(w, sid)

                @pl.when(z > 0)
                def _():
                    send(w, sid, down_dev, z_sem.at[w, 1, zz])

            spread(zz)

    def round_side(r):
        if r == 0:
            side(z)
            return

        @pl.when(z >= r)
        def _():
            side(z - r)

        @pl.when(z + r < LAYERS)
        def _():
            side(z + r)

    round_z(1)
    round_side(0)
    round_z(2)
    for d in range(1, WIN):
        a_copy(d).start()

    @pl.when(tm == 0)
    def _():
        lo_recv[...] = lo_send[0]
        for d in range(1, WIN):
            l_copy(d).start()

    round_side(1)
    round_z(3)
    round_side(2)
    round_side(3)
    for d in range(1, WIN):
        n_copy(d).start()

    def a_arrive(d):
        src = (tm + d) % WIN
        pltpu.make_async_remote_copy(
            src_ref=a_send.at[src, first], dst_ref=a_recv.at[src, first], send_sem=a_ssem.at[d],
            recv_sem=a_rsem.at[src], device_id=(src, bt), device_id_type=MESH,
        ).wait_recv()

    def n_arrive(d):
        src = (tm + d) % WIN
        pltpu.make_async_remote_copy(
            src_ref=a_send.at[src, second], dst_ref=a_recv.at[src, second], send_sem=n_ssem.at[d],
            recv_sem=n_rsem.at[src], device_id=(src, bt), device_id_type=MESH,
        ).wait_recv()

    for d in range(1, WIN):
        a_arrive(d)

    @pl.when(tm > 0)
    def _():
        l_copy(1).wait_recv()

    for j in range(WIN):
        cur[j] = a_recv[j, 0:part, :].astype(jnp.float32)

    def before_mlp(s):
        @pl.loop(0, WIN)
        def _(j):
            now = cur[j]
            centred = now - jnp.mean(now, axis=1, keepdims=True)
            var = jnp.mean(centred * centred, axis=1, keepdims=True)
            normed = centred * lax.rsqrt(var + EPSILON)
            shift = mod[pl.ds(s * WIN + j, 1), 0:width]
            scale = mod[pl.ds(s * WIN + j, 1), width : 2 * width]
            rows = pl.ds(pl.multiple_of(j * part, part), part)
            hid[rows, :] = (normed * (1.0 + scale) + shift).astype(jnp.bfloat16)
            acc[rows, :] = jnp.zeros((part, width), jnp.float32)

    def mlp(first, count):
        rows = pl.ds(pl.multiple_of(first, 128), count)
        before = lax.dot_general(
            hid[...], up_full[rows, :], (((1,), (1,)), ((), ())), preferred_element_type=jnp.float32
        )
        act = jax.nn.gelu(before, approximate=True).astype(jnp.bfloat16)
        acc[...] += jnp.dot(act, dn_full[rows, :], preferred_element_type=jnp.float32)

    def after_mlp(base):
        pre[0] = base
        for j in range(WIN):
            k = start + j
            rows = pl.ds(j * part, part)
            gate = mod[j : j + 1, 2 * width : 3 * width]
            noise = a_recv[j, part : 2 * part, :].astype(jnp.float32)
            pre[j + 1] = pre[j] + (dt_ref[k] * (gate * acc[rows, :] - cur[j]) + sg_ref[k] * noise)

    before_mlp(0)
    flip = z // 2
    near = z + flip * (3 - 2 * z)

    @pl.loop(0, LAYERS)
    def _(p):
        early = 1 - p // 2
        order = p + near * early * (1 - 2 * p)
        zz = order + flip * (3 - 2 * order)
        across = ident(zz, xn, yn, c)
        arrive(0, across)
        for k in (0, 1):
            piece_copy(k, across, s_dev, s_sem.at[1, 3, zz]).wait_recv()
        for w in (0, 1):
            send(w, across, s_dev, s_sem.at[w, 3, zz])
        for xx in (0, 1):
            for yy in (0, 1):
                for w in (0, 1):
                    arrive(w, ident(zz, xx, yy, cn))

        @pl.loop(0, 3)
        def _(i):
            mlp(zz * layer + i * (layer // 3), layer // 3)

    after_mlp(cur[0] + lo_recv[...].astype(jnp.float32))
    for j in range(WIN):
        cur[j] = pre[jnp.minimum(adv + j, WIN)]
    before_mlp(1)
    rows_used = (WIN - 1) * part
    hidden = LAYERS * layer

    @pl.loop(0, 3)
    def _(i):
        for k in range(3):
            rows = pl.ds(pl.multiple_of((i * 3 + k) * (hidden // 9), 128), hidden // 9)
            before = lax.dot_general(
                hid[0:rows_used, :], up_full[rows, :], (((1,), (1,)), ((), ())),
                preferred_element_type=jnp.float32,
            )
            act_all[:, rows] = jax.nn.gelu(before, approximate=True).astype(jnp.bfloat16)

    own_rows = pl.ds(pl.multiple_of(tm * part, part), part)

    def o_copy(b, d):
        to = (tm + d) % WIN
        return pltpu.make_async_remote_copy(
            src_ref=o_send.at[to, :, spans[b]], dst_ref=out_ref.at[own_rows, spans[b]],
            send_sem=o_ssem.at[b, d], recv_sem=o_rsem.at[b, tm],
            device_id=(to, bt), device_id_type=MESH,
        )

    def o_arrive(b, d):
        src = (tm + d) % WIN
        pltpu.make_async_remote_copy(
            src_ref=o_send.at[src, :, spans[b]],
            dst_ref=out_ref.at[pl.ds(pl.multiple_of(src * part, part), part), spans[b]],
            send_sem=o_ssem.at[b, d], recv_sem=o_rsem.at[b, src],
            device_id=(src, bt), device_id_type=MESH,
        ).wait_recv()

    for d in range(1, WIN):
        n_arrive(d)
    edges = tuple(width * e // 9 for e in SPLIT)
    spans = tuple(pl.ds(lo, hi - lo) for lo, hi in zip(edges, edges[1:]))
    for b, (lo, hi) in enumerate(zip(edges, edges[1:])):
        mlp_out = jnp.dot(act_all[...], dn_full[:, lo:hi], preferred_element_type=jnp.float32)
        total = cur[0, :, lo:hi]
        for j in range(WIN):
            o_send[j, :, lo:hi] = total.astype(jnp.bfloat16)
            if j == WIN - 1:
                break
            k = start + adv + j
            gate = mod[WIN + j : WIN + j + 1, 2 * width + lo : 2 * width + hi]
            noise = a_recv[j, 2 * part : 3 * part, lo:hi].astype(jnp.float32)
            drift = gate * mlp_out[j * part : (j + 1) * part] - cur[j, :, lo:hi]
            total = total + (dt_ref[k] * drift + sg_ref[k] * noise)
        for d in range(1, WIN):
            o_copy(b, d).start()
    mine = pltpu.make_async_copy(o_send.at[tm], out_ref.at[own_rows], loc_sem.at[0])
    mine.start()

    for zz in range(LAYERS):
        for w in (0, 1):
            @pl.when((z < LAYERS - 1) & (zz <= z))
            def _():
                sent(w, z_sem.at[w, 0, zz])

            @pl.when((z > 0) & (zz >= z))
            def _():
                sent(w, z_sem.at[w, 1, zz])

            sent(w, x_sem.at[w, 0, zz])
            sent(w, y_sem.at[w, 0, zz])
            for kind in range(4):
                sent(w, s_sem.at[w, kind, zz])
        sent(0, y_sem.at[0, 1, zz])
        piece_copy(1, 0, s_dev, x_sem.at[1, 1, zz]).wait_send()
        piece_copy(0, 0, s_dev, y_sem.at[1, 1, zz]).wait_send()
    for d in range(1, WIN):
        a_copy(d).wait_send()
        n_copy(d).wait_send()

    @pl.when(tm == 0)
    def _():
        for d in range(1, WIN):
            l_copy(d).wait_send()

    mine.wait()
    for b in range(len(spans)):
        for d in range(1, WIN):
            o_arrive(b, d)
            o_copy(b, d).wait_send()


def per_device_fused(
    state, noise_draws, class_vec, window_start, advance, step_dt, step_sigma, w_ada, w_up, w_down
):
    tokens, width = state.shape[2:]
    hidden = w_up.shape[0] * WIN * 4
    part = tokens // WIN
    bf16, f32 = jnp.bfloat16, jnp.float32
    vmem, smem = pl.BlockSpec(memory_space=pltpu.VMEM), pl.BlockSpec(memory_space=pltpu.SMEM)
    dma = pltpu.SemaphoreType.DMA
    flops = 2 * 2 * 2 * tokens * width * hidden
    out = pl.pallas_call(
        fused,
        out_shape=jax.ShapeDtypeStruct((tokens, width), bf16),
        in_specs=[smem] * 4 + [vmem] * 5 + [pl.BlockSpec(memory_space=pl.ANY)],
        out_specs=pl.BlockSpec(memory_space=pl.ANY),
        scratch_shapes=[
            pltpu.VMEM((hidden, width), bf16),
            pltpu.VMEM((hidden, width), bf16),
            pltpu.VMEM(w_ada.shape, bf16),
            pltpu.VMEM((2 * WIN, 3 * width), f32),
            pltpu.VMEM((WIN, 3 * part, width), bf16),
            pltpu.VMEM((WIN, 3 * part, width), bf16),
            pltpu.VMEM((WIN, part, width), bf16),
            pltpu.VMEM((part, width), bf16),
            pltpu.VMEM((WIN, part, width), f32),
            pltpu.VMEM((tokens, width), bf16),
            pltpu.VMEM((tokens, width), f32),
            pltpu.VMEM((WIN + 1, part, width), f32),
            pltpu.VMEM((WIN, part, width), bf16),
            pltpu.VMEM(((WIN - 1) * part, hidden), bf16),
            dma((3,)),
            dma((3, 32)),
            dma((2, 2, LAYERS)),
            dma((2, 2, LAYERS)),
            dma((2, 2, LAYERS)),
            dma((2, 4, LAYERS)),
            dma((WIN,)),
            dma((WIN,)),
            dma((WIN,)),
            dma((WIN,)),
            dma((WIN,)),
            dma,
            dma((len(SPLIT) - 1, WIN)),
            dma((len(SPLIT) - 1, WIN)),
        ],
        compiler_params=pltpu.CompilerParams(
            collective_id=0, has_side_effects=True, vmem_limit_bytes=58 * 2**20
        ),
        cost_estimate=pl.CostEstimate(flops=flops, bytes_accessed=2 * w_ada.size, transcendentals=0),
        name="picard",
    )(
        window_start, advance, step_dt, step_sigma, class_vec,
        state[0, 0], noise_draws[:, 0, 0], w_up, w_down, w_ada,
    )
    return out.astype(f32)[None, None]


def solution(mesh):
    in_specs = (
        P("tm", "batch", None, None),
        P(None, "tm", "batch", None, None),
        P("batch", None),
        P("batch"),
        P("batch"),
        P(),
        P(),
        P(),
        P(("tm", "batch"), None),
        P(("tm", "batch"), None),
    )
    out_specs = P("tm", "batch", None, None)
    small = mesh.shape["tm"] == WIN and mesh.shape["batch"] == 4
    return jax.shard_map(
        per_device_fused if small else per_device,
        mesh=mesh, in_specs=in_specs, out_specs=out_specs, check_vma=False,
    )
```

```python
import functools
import math

import jax
import jax.numpy as jnp
from jax import lax
from jax.experimental import pallas as pl
from jax.experimental.pallas import tpu as pltpu
from jax.sharding import PartitionSpec as P

SLIDE_BITS = 3
MESH = pl.DeviceIdType.MESH
WIN = 8
LAYERS = 4

EPSILON = 1e-06


def spread_2(shard, axis, root):
    mine = lax.axis_index(axis) == root
    return lax.psum(jnp.where(mine, shard, jnp.zeros_like(shard)), axis)


def carried_in(part, axis, combine, identity):
    place = lax.axis_index(axis)
    gathered = lax.all_gather(part, axis)
    state = jnp.zeros_like(part) + jnp.asarray(identity, part.dtype)

    def one(turn, state):
        return combine(state, lax.dynamic_index_in_dim(gathered, turn, 0, False))

    return lax.fori_loop(0, place, one, state)


def from_behind(shard, axis, by):
    peers = lax.axis_size(axis)
    pairs = [(i, i + by) for i in range(peers) if 0 <= i + by < peers]
    return lax.ppermute(shard, axis, pairs)


def time_embed(steps_now, half_width):
    frequency = jnp.exp(-math.log(10000.0) * jnp.arange(half_width, dtype=jnp.float32) / half_width)
    angles = steps_now.astype(jnp.float32)[:, None] * frequency[None, :]
    return jnp.concatenate([jnp.cos(angles), jnp.sin(angles)], axis=1)


def dense_pair(hidden_rows, up_rows, down_rows):
    before = lax.dot_general(
        hidden_rows, up_rows, (((1,), (1,)), ((), ())), preferred_element_type=jnp.float32
    )
    activated = jax.nn.gelu(before, approximate=True).astype(jnp.bfloat16)
    return jnp.dot(activated, down_rows, preferred_element_type=jnp.float32)


def combine_sum(earlier, later):
    return earlier + later


def increment(current, noise_now, steps_now, class_vec, step_dt, step_sigma, w_ada, mlp_apply):
    images, tokens, channels = current.shape
    step_table = lax.iota(jnp.int32, step_dt.shape[0])
    onehot = (steps_now[:, None] == step_table[None, :]).astype(jnp.float32)
    step_size = jnp.sum(onehot * step_dt[None, :], axis=1)
    spread = jnp.sum(onehot * step_sigma[None, :], axis=1)
    condition = jax.nn.silu(time_embed(steps_now, channels // 2) + class_vec).astype(jnp.bfloat16)
    modulation = jnp.dot(condition, w_ada, preferred_element_type=jnp.float32)
    shift_by = modulation[:, :channels]
    scale_by = modulation[:, channels : 2 * channels]
    gate_by = modulation[:, 2 * channels :]
    mean_val = jnp.mean(current, axis=2, keepdims=True)
    centred = current - mean_val
    var_val = jnp.mean(centred * centred, axis=2, keepdims=True)
    normed = centred * lax.rsqrt(var_val + EPSILON)
    hidden_in = (normed * (1.0 + scale_by[:, None, :]) + shift_by[:, None, :]).astype(jnp.bfloat16)
    mlp_out = mlp_apply(hidden_in.reshape(images * tokens, channels)).reshape(
        images, tokens, channels
    )
    drift = gate_by[:, None, :] * mlp_out - current
    return step_size[:, None, None] * drift + spread[:, None, None] * noise_now.astype(jnp.float32)


def per_device(
    state, noise_draws, class_vec, window_start, advance, step_dt, step_sigma, w_ada, w_up, w_down
):
    window_size = lax.axis_size("tm")
    position = lax.axis_index("tm")
    up_whole, down_whole = (
        lax.all_gather(w_up, ("tm", "batch"), axis=0, tiled=True),
        lax.all_gather(w_down, ("tm", "batch"), axis=0, tiled=True),
    )

    def mlp_apply(hidden_rows):
        return dense_pair(hidden_rows, up_whole, down_whole)

    def sweep(current, noise_now, starts):
        steps_now = starts + position
        step_inc = increment(
            current, noise_now, steps_now, class_vec, step_dt, step_sigma, w_ada, mlp_apply
        )
        base_rows = spread_2(current, "tm", 0)
        prefix = carried_in(step_inc, "tm", combine_sum, jnp.zeros_like(step_inc))
        updated = base_rows + prefix
        return (updated, step_inc)

    updated, step_inc = sweep(state[0], noise_draws[0, 0], window_start)
    end_rows = updated + step_inc
    tail_rows = jnp.where(position == window_size - 1, end_rows, jnp.zeros_like(end_rows))
    moved = updated
    for section_bit in range(SLIDE_BITS):
        distance = 1 << section_bit
        arrived, arrived_tail = from_behind((moved, tail_rows), "tm", -distance)
        taken = advance >> section_bit & 1 == 1
        outside = position + distance >= window_size
        incoming = jnp.where(outside, tail_rows, arrived)
        moved = jnp.where(taken[:, None, None], incoming, moved)
        tail_rows = jnp.where(position >= window_size - distance, tail_rows, arrived_tail)
    final_rows, leftover = sweep(moved, noise_draws[1, 0], window_start + advance)
    return final_rows[None]


SPLIT = (0, 2, 6, 9)
LATE = 2
TURNED = 1


def fused(
    start_ref, adv_ref, dt_ref, sg_ref, cls_ref, state_ref, noise_ref, wup_ref, wdn_ref, wada_ref,
    out_ref,
    up_full, dn_full, ada_buf, mod, a_send, a_recv, lo_send, lo_recv, cur, hid, acc, pre, o_send, act_all,
    loc_sem, w_recv, z_sem, r_sem, x_sem, y_sem, s_sem, a_ssem, a_rsem, n_ssem, n_rsem, l_ssem, l_rsem, o_ssem, o_rsem,
):
    tokens, width = state_ref.shape
    part = tokens // WIN
    depth = wup_ref.shape[0]
    layer = 8 * depth
    tm, bt = lax.axis_index("tm"), lax.axis_index("batch")
    z, x = tm // 2, tm % 2
    y, c = bt // 2, bt % 2
    xn, yn, cn = 1 - x, 1 - y, 1 - c

    def dev(zz, xx, yy, cc):
        return (zz * 2 + xx, yy * 2 + cc)

    x_dev, y_dev, s_dev = dev(z, xn, y, c), dev(z, x, yn, c), dev(z, x, y, cn)
    up_dev, down_dev = dev(z + 1, x, y, c), dev(z - 1, x, y, c)

    barrier = pltpu.get_barrier_semaphore()
    for d in range(1, WIN):
        pl.semaphore_signal(barrier, inc=1, device_id=((tm + d) % WIN, bt), device_id_type=MESH)
    pl.semaphore_signal(barrier, inc=1, device_id=y_dev, device_id_type=MESH)
    pl.semaphore_signal(barrier, inc=1, device_id=s_dev, device_id_type=MESH)
    pl.semaphore_wait(barrier, WIN + 1)

    late = depth * LATE // 9 // 16 * 16
    pieces = (
        (wup_ref, up_full, 0, depth), (wdn_ref, dn_full, 0, depth - late), (wdn_ref, dn_full, depth - late, late),
    )

    def block(w, sid):
        _, full, lo, count = pieces[w]
        return full.at[pl.ds(pl.multiple_of(sid * depth + lo, 16), count)]

    def given(w):
        ref, _, lo, count = pieces[w]
        return ref.at[pl.ds(lo, count)]

    def ident(zz, xx, yy, cc):
        return (zz * 2 + xx) * 4 + yy * 2 + cc

    def send(w, sid, to, sem, own=False):
        pltpu.make_async_remote_copy(
            src_ref=given(w) if own else block(w, sid), dst_ref=block(w, sid),
            send_sem=sem, recv_sem=w_recv.at[w, sid], device_id=to, device_id_type=MESH,
        ).start()

    def arrive(w, sid):
        pltpu.make_async_remote_copy(
            src_ref=block(w, sid), dst_ref=block(w, sid),
            send_sem=s_sem.at[w, 0, 0], recv_sem=w_recv.at[w, sid], device_id=s_dev, device_id_type=MESH,
        ).wait_recv()

    turned = depth * TURNED // 9 // 16 * 16
    cuts = ((0, turned), (turned, depth - late - turned))

    def piece(k, sid):
        return dn_full.at[pl.ds(pl.multiple_of(sid * depth + cuts[k][0], 16), cuts[k][1])]

    def piece_copy(k, sid, to, sem):
        return pltpu.make_async_remote_copy(
            src_ref=piece(k, sid), dst_ref=piece(k, sid),
            send_sem=sem, recv_sem=w_recv.at[1 + 2 * k, sid], device_id=to, device_id_type=MESH,
        )

    def sent(w, sem):
        pltpu.make_async_remote_copy(
            src_ref=given(w), dst_ref=block(w, 0),
            send_sem=sem, recv_sem=w_recv.at[w, 0], device_id=s_dev, device_id_type=MESH,
        ).wait_send()

    def spread(zz, own=False):
        sid = ident(zz, x, y, c)
        for w in (0, 1):
            send(w, sid, x_dev, x_sem.at[w, 0, zz], own)
            send(w, sid, y_dev, y_sem.at[w, 0, zz], own)
        for w in (0, 1):
            send(w, sid, s_dev, s_sem.at[w, 0, zz], own)

    def side(zz):
        from_x, from_y = ident(zz, xn, y, c), ident(zz, x, yn, c)
        arrive(0, from_x)
        send(0, from_x, y_dev, y_sem.at[0, 1, zz])
        arrive(1, from_y)
        piece_copy(1, from_y, x_dev, x_sem.at[1, 1, zz]).start()
        arrive(1, from_x)
        piece_copy(0, from_x, y_dev, y_sem.at[1, 1, zz]).start()
        arrive(0, from_y)
        for w in (0, 1):
            send(w, from_x, s_dev, s_sem.at[w, 1, zz])
            send(w, from_y, s_dev, s_sem.at[w, 2, zz])

    def columns_of(zz):
        return (ident(zz, x, y, c), ident(zz, xn, y, c), ident(zz, x, yn, c), ident(zz, xn, yn, c))

    def late_on(zz, kind, up, down, own=False):
        sid = columns_of(zz)[kind]
        if up:
            @pl.when(z < LAYERS - 1)
            def _():
                send(2, sid, up_dev, r_sem.at[0, kind, zz], own)
        if down:
            @pl.when(z > 0)
            def _():
                send(2, sid, down_dev, r_sem.at[1, kind, zz], own)
        if not own:
            send(2, sid, s_dev, s_sem.at[2, kind, zz])

    def late_layer():
        mine_, from_x, from_y, across = columns_of(z)
        late_on(z, 0, True, True, True)
        arrive(2, from_x)
        send(2, from_x, y_dev, y_sem.at[2, 1, z])
        late_on(z, 1, True, True)
        arrive(2, from_y)
        late_on(z, 2, True, True)
        arrive(2, across)
        late_on(z, 3, True, True)

    def late_z(r):
        @pl.when(z >= r)
        def _():
            for kind in range(4):
                arrive(2, columns_of(z - r)[kind])
                late_on(z - r, kind, True, False)

        @pl.when(z + r < LAYERS)
        def _():
            for kind in range(4):
                arrive(2, columns_of(z + r)[kind])
                late_on(z + r, kind, False, True)

    me = ident(z, x, y, c)

    @pl.when(z < LAYERS - 1)
    def _():
        for w in (0, 1):
            send(w, me, up_dev, z_sem.at[w, 0, z], True)

    @pl.when(z > 0)
    def _():
        for w in (0, 1):
            send(w, me, down_dev, z_sem.at[w, 1, z], True)

    spread(z, True)
    send(2, me, x_dev, x_sem.at[2, 0, z], True)
    send(2, me, y_dev, y_sem.at[2, 0, z], True)
    send(2, me, s_dev, s_sem.at[2, 0, z], True)
    local = [
        pltpu.make_async_copy(wada_ref, ada_buf, loc_sem.at[0]),
        pltpu.make_async_copy(given(0), block(0, me), loc_sem.at[1]),
        pltpu.make_async_copy(given(1), block(1, me), loc_sem.at[2]),
        pltpu.make_async_copy(given(2), block(2, me), loc_sem.at[3]),
    ]
    for copy in local:
        copy.start()

    for t in range(WIN):
        rows = pl.ds(t * part, part)
        whole = state_ref[rows, :]
        high = whole.astype(jnp.bfloat16)
        a_send[t, 0:part, :] = high
        lo_send[t] = (whole - high.astype(jnp.float32)).astype(jnp.bfloat16)
        a_send[t, part : 2 * part, :] = noise_ref[0, rows, :]
        a_send[t, 2 * part : 3 * part, :] = noise_ref[1, rows, :]
    a_recv[tm] = a_send[tm]

    start, adv = start_ref[0], adv_ref[0]
    row = lax.broadcasted_iota(jnp.int32, (2 * WIN, width), 0)
    lane = lax.broadcasted_iota(jnp.int32, (2 * WIN, width), 1)
    half = width // 2
    second_sweep = row >= WIN
    steps = (start + jnp.where(second_sweep, adv + row - WIN, row)).astype(jnp.float32)
    turn = jnp.where(lane >= half, lane - half, lane).astype(jnp.float32)
    angles = steps * jnp.exp(-math.log(10000.0) * turn / half)
    embed = jnp.where(lane >= half, jnp.sin(angles), jnp.cos(angles))
    condition = jax.nn.silu(embed + cls_ref[...]).astype(jnp.bfloat16)
    for copy in local:
        copy.wait()
    for third in range(3):
        columns = slice(third * width, (third + 1) * width)
        mod[:, columns] = jnp.dot(condition, ada_buf[:, columns], preferred_element_type=jnp.float32)

    first, second = pl.ds(0, 2 * part), pl.ds(2 * part, part)

    def a_copy(d):
        to = (tm + d) % WIN
        return pltpu.make_async_remote_copy(
            src_ref=a_send.at[to, first], dst_ref=a_recv.at[tm, first], send_sem=a_ssem.at[d],
            recv_sem=a_rsem.at[tm], device_id=(to, bt), device_id_type=MESH,
        )

    def n_copy(d):
        to = (tm + d) % WIN
        return pltpu.make_async_remote_copy(
            src_ref=a_send.at[to, second], dst_ref=a_recv.at[tm, second], send_sem=n_ssem.at[d],
            recv_sem=n_rsem.at[tm], device_id=(to, bt), device_id_type=MESH,
        )

    def l_copy(d):
        return pltpu.make_async_remote_copy(
            src_ref=lo_send.at[d], dst_ref=lo_recv, send_sem=l_ssem.at[d],
            recv_sem=l_rsem, device_id=(d, bt), device_id_type=MESH,
        )

    def round_z(r):
        @pl.when(z >= r)
        def _():
            zz = z - r
            sid = ident(zz, x, y, c)
            for w in (0, 1):
                arrive(w, sid)

                @pl.when(z < LAYERS - 1)
                def _():
                    send(w, sid, up_dev, z_sem.at[w, 0, zz])

            spread(zz)

        @pl.when(z + r < LAYERS)
        def _():
            zz = z + r
            sid = ident(zz, x, y, c)
            for w in (0, 1):
                arrive(w, sid)

                @pl.when(z > 0)
                def _():
                    send(w, sid, down_dev, z_sem.at[w, 1, zz])

            spread(zz)

    def round_side(r):
        if r == 0:
            side(z)
            return

        @pl.when(z >= r)
        def _():
            side(z - r)

        @pl.when(z + r < LAYERS)
        def _():
            side(z + r)

    round_z(1)
    round_side(0)
    late_layer()
    round_z(2)
    for d in range(1, WIN):
        a_copy(d).start()

    @pl.when(tm == 0)
    def _():
        lo_recv[...] = lo_send[0]
        for d in range(1, WIN):
            l_copy(d).start()

    round_side(1)
    late_z(1)
    round_z(3)
    late_z(2)
    round_side(2)

    def a_arrive(d):
        src = (tm + d) % WIN
        pltpu.make_async_remote_copy(
            src_ref=a_send.at[src, first], dst_ref=a_recv.at[src, first], send_sem=a_ssem.at[d],
            recv_sem=a_rsem.at[src], device_id=(src, bt), device_id_type=MESH,
        ).wait_recv()

    def n_arrive(d):
        src = (tm + d) % WIN
        pltpu.make_async_remote_copy(
            src_ref=a_send.at[src, second], dst_ref=a_recv.at[src, second], send_sem=n_ssem.at[d],
            recv_sem=n_rsem.at[src], device_id=(src, bt), device_id_type=MESH,
        ).wait_recv()

    def before_mlp(s):
        @pl.loop(0, WIN)
        def _(j):
            now = cur[j]
            centred = now - jnp.mean(now, axis=1, keepdims=True)
            var = jnp.mean(centred * centred, axis=1, keepdims=True)
            normed = centred * lax.rsqrt(var + EPSILON)
            shift = mod[pl.ds(s * WIN + j, 1), 0:width]
            scale = mod[pl.ds(s * WIN + j, 1), width : 2 * width]
            rows = pl.ds(pl.multiple_of(j * part, part), part)
            hid[rows, :] = (normed * (1.0 + scale) + shift).astype(jnp.bfloat16)
            acc[rows, :] = jnp.zeros((part, width), jnp.float32)

    def mlp(first, count):
        rows = pl.ds(pl.multiple_of(first, 128), count)
        before = lax.dot_general(
            hid[...], up_full[rows, :], (((1,), (1,)), ((), ())), preferred_element_type=jnp.float32
        )
        act = jax.nn.gelu(before, approximate=True).astype(jnp.bfloat16)
        acc[...] += jnp.dot(act, dn_full[rows, :], preferred_element_type=jnp.float32)

    def after_mlp(base):
        pre[0] = base
        for j in range(WIN):
            k = start + j
            rows = pl.ds(j * part, part)
            gate = mod[j : j + 1, 2 * width : 3 * width]
            noise = a_recv[j, part : 2 * part, :].astype(jnp.float32)
            pre[j + 1] = pre[j] + (dt_ref[k] * (gate * acc[rows, :] - cur[j]) + sg_ref[k] * noise)

    for d in range(1, WIN):
        a_arrive(d)

    @pl.when(tm > 0)
    def _():
        l_copy(1).wait_recv()

    for j in range(WIN):
        cur[j] = a_recv[j, 0:part, :].astype(jnp.float32)

    before_mlp(0)
    flip = z // 2
    near = z + flip * (3 - 2 * z)

    def through(p):
        early = 1 - p // 2
        order = p + near * early * (1 - 2 * p)
        zz = order + flip * (3 - 2 * order)
        across = ident(zz, xn, yn, c)
        arrive(0, across)
        for k in (0, 1):
            piece_copy(k, across, s_dev, s_sem.at[1, 3, zz]).wait_recv()
        for w in (0, 1):
            send(w, across, s_dev, s_sem.at[w, 3, zz])
        for xx in (0, 1):
            for yy in (0, 1):
                for w in (0, 1, 2):
                    arrive(w, ident(zz, xx, yy, cn))

        @pl.loop(0, 3)
        def _(i):
            mlp(zz * layer + i * (layer // 3), layer // 3)

    pl.loop(0, 2)(through)
    late_z(3)
    round_side(3)
    for d in range(1, WIN):
        n_copy(d).start()
    pl.loop(2, LAYERS)(through)
    after_mlp(cur[0] + lo_recv[...].astype(jnp.float32))
    for j in range(WIN):
        cur[j] = pre[jnp.minimum(adv + j, WIN)]
    before_mlp(1)
    rows_used = (WIN - 1) * part
    hidden = LAYERS * layer

    @pl.loop(0, 3)
    def _(i):
        for k in range(3):
            rows = pl.ds(pl.multiple_of((i * 3 + k) * (hidden // 9), 128), hidden // 9)
            before = lax.dot_general(
                hid[0:rows_used, :], up_full[rows, :], (((1,), (1,)), ((), ())),
                preferred_element_type=jnp.float32,
            )
            act_all[:, rows] = jax.nn.gelu(before, approximate=True).astype(jnp.bfloat16)

    own_rows = pl.ds(pl.multiple_of(tm * part, part), part)

    def o_copy(b, d):
        to = (tm + d) % WIN
        return pltpu.make_async_remote_copy(
            src_ref=o_send.at[to, :, spans[b]], dst_ref=out_ref.at[own_rows, spans[b]],
            send_sem=o_ssem.at[b, d], recv_sem=o_rsem.at[b, tm],
            device_id=(to, bt), device_id_type=MESH,
        )

    def o_arrive(b, d):
        src = (tm + d) % WIN
        pltpu.make_async_remote_copy(
            src_ref=o_send.at[src, :, spans[b]],
            dst_ref=out_ref.at[pl.ds(pl.multiple_of(src * part, part), part), spans[b]],
            send_sem=o_ssem.at[b, d], recv_sem=o_rsem.at[b, src],
            device_id=(src, bt), device_id_type=MESH,
        ).wait_recv()

    for d in range(1, WIN):
        n_arrive(d)
    edges = tuple(width * e // 9 for e in SPLIT)
    spans = tuple(pl.ds(lo, hi - lo) for lo, hi in zip(edges, edges[1:]))
    for b, (lo, hi) in enumerate(zip(edges, edges[1:])):
        mlp_out = jnp.dot(act_all[...], dn_full[:, lo:hi], preferred_element_type=jnp.float32)
        total = cur[0, :, lo:hi]
        for j in range(WIN):
            o_send[j, :, lo:hi] = total.astype(jnp.bfloat16)
            if j == WIN - 1:
                break
            k = start + adv + j
            gate = mod[WIN + j : WIN + j + 1, 2 * width + lo : 2 * width + hi]
            noise = a_recv[j, 2 * part : 3 * part, lo:hi].astype(jnp.float32)
            drift = gate * mlp_out[j * part : (j + 1) * part] - cur[j, :, lo:hi]
            total = total + (dt_ref[k] * drift + sg_ref[k] * noise)
        for d in range(1, WIN):
            o_copy(b, d).start()
    mine = pltpu.make_async_copy(o_send.at[tm], out_ref.at[own_rows], loc_sem.at[0])
    mine.start()

    sent(2, x_sem.at[2, 0, z])
    sent(2, y_sem.at[2, 0, z])
    sent(2, y_sem.at[2, 1, z])
    for zz in range(LAYERS):
        for w in (0, 1):
            @pl.when((z < LAYERS - 1) & (zz <= z))
            def _():
                sent(w, z_sem.at[w, 0, zz])

            @pl.when((z > 0) & (zz >= z))
            def _():
                sent(w, z_sem.at[w, 1, zz])

            sent(w, x_sem.at[w, 0, zz])
            sent(w, y_sem.at[w, 0, zz])
        for w in (0, 1, 2):
            for kind in range(4):
                sent(w, s_sem.at[w, kind, zz])
        for kind in range(4):
            @pl.when((z < LAYERS - 1) & (zz <= z))
            def _():
                sent(2, r_sem.at[0, kind, zz])

            @pl.when((z > 0) & (zz >= z))
            def _():
                sent(2, r_sem.at[1, kind, zz])

        sent(0, y_sem.at[0, 1, zz])
        piece_copy(1, 0, s_dev, x_sem.at[1, 1, zz]).wait_send()
        piece_copy(0, 0, s_dev, y_sem.at[1, 1, zz]).wait_send()
    for d in range(1, WIN):
        a_copy(d).wait_send()
        n_copy(d).wait_send()

    @pl.when(tm == 0)
    def _():
        for d in range(1, WIN):
            l_copy(d).wait_send()

    mine.wait()
    for b in range(len(spans)):
        for d in range(1, WIN):
            o_arrive(b, d)
            o_copy(b, d).wait_send()


def per_device_fused(
    state, noise_draws, class_vec, window_start, advance, step_dt, step_sigma, w_ada, w_up, w_down
):
    tokens, width = state.shape[2:]
    hidden = w_up.shape[0] * WIN * 4
    part = tokens // WIN
    bf16, f32 = jnp.bfloat16, jnp.float32
    vmem, smem = pl.BlockSpec(memory_space=pltpu.VMEM), pl.BlockSpec(memory_space=pltpu.SMEM)
    dma = pltpu.SemaphoreType.DMA
    flops = 2 * 2 * 2 * tokens * width * hidden
    out = pl.pallas_call(
        fused,
        out_shape=jax.ShapeDtypeStruct((tokens, width), bf16),
        in_specs=[smem] * 4 + [vmem] * 5 + [pl.BlockSpec(memory_space=pl.ANY)],
        out_specs=pl.BlockSpec(memory_space=pl.ANY),
        scratch_shapes=[
            pltpu.VMEM((hidden, width), bf16),
            pltpu.VMEM((hidden, width), bf16),
            pltpu.VMEM(w_ada.shape, bf16),
            pltpu.VMEM((2 * WIN, 3 * width), f32),
            pltpu.VMEM((WIN, 3 * part, width), bf16),
            pltpu.VMEM((WIN, 3 * part, width), bf16),
            pltpu.VMEM((WIN, part, width), bf16),
            pltpu.VMEM((part, width), bf16),
            pltpu.VMEM((WIN, part, width), f32),
            pltpu.VMEM((tokens, width), bf16),
            pltpu.VMEM((tokens, width), f32),
            pltpu.VMEM((WIN + 1, part, width), f32),
            pltpu.VMEM((WIN, part, width), bf16),
            pltpu.VMEM(((WIN - 1) * part, hidden), bf16),
            dma((4,)),
            dma((4, 32)),
            dma((2, 2, LAYERS)),
            dma((2, 4, LAYERS)),
            dma((3, 2, LAYERS)),
            dma((3, 2, LAYERS)),
            dma((3, 4, LAYERS)),
            dma((WIN,)),
            dma((WIN,)),
            dma((WIN,)),
            dma((WIN,)),
            dma((WIN,)),
            dma,
            dma((len(SPLIT) - 1, WIN)),
            dma((len(SPLIT) - 1, WIN)),
        ],
        compiler_params=pltpu.CompilerParams(
            collective_id=0, has_side_effects=True, vmem_limit_bytes=58 * 2**20
        ),
        cost_estimate=pl.CostEstimate(flops=flops, bytes_accessed=2 * w_ada.size, transcendentals=0),
        name="picard",
    )(
        window_start, advance, step_dt, step_sigma, class_vec,
        state[0, 0], noise_draws[:, 0, 0], w_up, w_down, w_ada,
    )
    return out.astype(f32)[None, None]


def solution(mesh):
    in_specs = (
        P("tm", "batch", None, None),
        P(None, "tm", "batch", None, None),
        P("batch", None),
        P("batch"),
        P("batch"),
        P(),
        P(),
        P(),
        P(("tm", "batch"), None),
        P(("tm", "batch"), None),
    )
    out_specs = P("tm", "batch", None, None)
    small = mesh.shape["tm"] == WIN and mesh.shape["batch"] == 4
    return jax.shard_map(
        per_device_fused if small else per_device,
        mesh=mesh, in_specs=in_specs, out_specs=out_specs, check_vma=False,
    )
```

```python
import functools
import math

import jax
import jax.numpy as jnp
from jax import lax
from jax.experimental import pallas as pl
from jax.experimental.pallas import tpu as pltpu
from jax.sharding import PartitionSpec as P

SLIDE_BITS = 3
MESH = pl.DeviceIdType.MESH
WIN = 8
LAYERS = 4

EPSILON = 1e-06


def spread_2(shard, axis, root):
    mine = lax.axis_index(axis) == root
    return lax.psum(jnp.where(mine, shard, jnp.zeros_like(shard)), axis)


def carried_in(part, axis, combine, identity):
    place = lax.axis_index(axis)
    gathered = lax.all_gather(part, axis)
    state = jnp.zeros_like(part) + jnp.asarray(identity, part.dtype)

    def one(turn, state):
        return combine(state, lax.dynamic_index_in_dim(gathered, turn, 0, False))

    return lax.fori_loop(0, place, one, state)


def from_behind(shard, axis, by):
    peers = lax.axis_size(axis)
    pairs = [(i, i + by) for i in range(peers) if 0 <= i + by < peers]
    return lax.ppermute(shard, axis, pairs)


def time_embed(steps_now, half_width):
    frequency = jnp.exp(-math.log(10000.0) * jnp.arange(half_width, dtype=jnp.float32) / half_width)
    angles = steps_now.astype(jnp.float32)[:, None] * frequency[None, :]
    return jnp.concatenate([jnp.cos(angles), jnp.sin(angles)], axis=1)


def dense_pair(hidden_rows, up_rows, down_rows):
    before = lax.dot_general(
        hidden_rows, up_rows, (((1,), (1,)), ((), ())), preferred_element_type=jnp.float32
    )
    activated = jax.nn.gelu(before, approximate=True).astype(jnp.bfloat16)
    return jnp.dot(activated, down_rows, preferred_element_type=jnp.float32)


def combine_sum(earlier, later):
    return earlier + later


def increment(current, noise_now, steps_now, class_vec, step_dt, step_sigma, w_ada, mlp_apply):
    images, tokens, channels = current.shape
    step_table = lax.iota(jnp.int32, step_dt.shape[0])
    onehot = (steps_now[:, None] == step_table[None, :]).astype(jnp.float32)
    step_size = jnp.sum(onehot * step_dt[None, :], axis=1)
    spread = jnp.sum(onehot * step_sigma[None, :], axis=1)
    condition = jax.nn.silu(time_embed(steps_now, channels // 2) + class_vec).astype(jnp.bfloat16)
    modulation = jnp.dot(condition, w_ada, preferred_element_type=jnp.float32)
    shift_by = modulation[:, :channels]
    scale_by = modulation[:, channels : 2 * channels]
    gate_by = modulation[:, 2 * channels :]
    mean_val = jnp.mean(current, axis=2, keepdims=True)
    centred = current - mean_val
    var_val = jnp.mean(centred * centred, axis=2, keepdims=True)
    normed = centred * lax.rsqrt(var_val + EPSILON)
    hidden_in = (normed * (1.0 + scale_by[:, None, :]) + shift_by[:, None, :]).astype(jnp.bfloat16)
    mlp_out = mlp_apply(hidden_in.reshape(images * tokens, channels)).reshape(
        images, tokens, channels
    )
    drift = gate_by[:, None, :] * mlp_out - current
    return step_size[:, None, None] * drift + spread[:, None, None] * noise_now.astype(jnp.float32)


def per_device(
    state, noise_draws, class_vec, window_start, advance, step_dt, step_sigma, w_ada, w_up, w_down
):
    window_size = lax.axis_size("tm")
    position = lax.axis_index("tm")
    up_whole, down_whole = (
        lax.all_gather(w_up, ("tm", "batch"), axis=0, tiled=True),
        lax.all_gather(w_down, ("tm", "batch"), axis=0, tiled=True),
    )

    def mlp_apply(hidden_rows):
        return dense_pair(hidden_rows, up_whole, down_whole)

    def sweep(current, noise_now, starts):
        steps_now = starts + position
        step_inc = increment(
            current, noise_now, steps_now, class_vec, step_dt, step_sigma, w_ada, mlp_apply
        )
        base_rows = spread_2(current, "tm", 0)
        prefix = carried_in(step_inc, "tm", combine_sum, jnp.zeros_like(step_inc))
        updated = base_rows + prefix
        return (updated, step_inc)

    updated, step_inc = sweep(state[0], noise_draws[0, 0], window_start)
    end_rows = updated + step_inc
    tail_rows = jnp.where(position == window_size - 1, end_rows, jnp.zeros_like(end_rows))
    moved = updated
    for section_bit in range(SLIDE_BITS):
        distance = 1 << section_bit
        arrived, arrived_tail = from_behind((moved, tail_rows), "tm", -distance)
        taken = advance >> section_bit & 1 == 1
        outside = position + distance >= window_size
        incoming = jnp.where(outside, tail_rows, arrived)
        moved = jnp.where(taken[:, None, None], incoming, moved)
        tail_rows = jnp.where(position >= window_size - distance, tail_rows, arrived_tail)
    final_rows, leftover = sweep(moved, noise_draws[1, 0], window_start + advance)
    return final_rows[None]


SPLIT = (0, 2, 6, 9)
TURNED = 2


def fused(
    start_ref, adv_ref, dt_ref, sg_ref, cls_ref, state_ref, noise_ref, wup_ref, wdn_ref, wada_ref,
    out_ref,
    up_full, dn_full, ada_buf, mod, a_send, a_recv, lo_send, lo_recv, cur, hid, acc, pre, o_send, act_all,
    loc_sem, w_recv, z_sem, x_sem, y_sem, s_sem, a_ssem, a_rsem, n_ssem, n_rsem, l_ssem, l_rsem, o_ssem, o_rsem,
):
    tokens, width = state_ref.shape
    part = tokens // WIN
    depth = wup_ref.shape[0]
    layer = 8 * depth
    tm, bt = lax.axis_index("tm"), lax.axis_index("batch")
    z, x = tm // 2, tm % 2
    y, c = bt // 2, bt % 2
    xn, yn, cn = 1 - x, 1 - y, 1 - c

    def dev(zz, xx, yy, cc):
        return (zz * 2 + xx, yy * 2 + cc)

    x_dev, y_dev, s_dev = dev(z, xn, y, c), dev(z, x, yn, c), dev(z, x, y, cn)
    up_dev, down_dev = dev(z + 1, x, y, c), dev(z - 1, x, y, c)

    barrier = pltpu.get_barrier_semaphore()
    for d in range(1, WIN):
        pl.semaphore_signal(barrier, inc=1, device_id=((tm + d) % WIN, bt), device_id_type=MESH)
    pl.semaphore_signal(barrier, inc=1, device_id=y_dev, device_id_type=MESH)
    pl.semaphore_signal(barrier, inc=1, device_id=s_dev, device_id_type=MESH)
    pl.semaphore_wait(barrier, WIN + 1)

    full = (up_full, dn_full)
    given = (wup_ref, wdn_ref)

    def block(w, sid):
        return full[w].at[pl.ds(pl.multiple_of(sid * depth, 16), depth)]

    def ident(zz, xx, yy, cc):
        return (zz * 2 + xx) * 4 + yy * 2 + cc

    def send(w, sid, to, sem, own=False):
        pltpu.make_async_remote_copy(
            src_ref=given[w] if own else block(w, sid), dst_ref=block(w, sid),
            send_sem=sem, recv_sem=w_recv.at[w, sid], device_id=to, device_id_type=MESH,
        ).start()

    def arrive(w, sid):
        pltpu.make_async_remote_copy(
            src_ref=block(w, sid), dst_ref=block(w, sid),
            send_sem=s_sem.at[w, 0, 0], recv_sem=w_recv.at[w, sid], device_id=s_dev, device_id_type=MESH,
        ).wait_recv()

    turned = depth * TURNED // 9 // 16 * 16
    cuts = ((0, turned), (turned, depth - turned))

    def piece(k, sid):
        return dn_full.at[pl.ds(pl.multiple_of(sid * depth + cuts[k][0], 16), cuts[k][1])]

    def piece_copy(k, sid, to, sem):
        return pltpu.make_async_remote_copy(
            src_ref=piece(k, sid), dst_ref=piece(k, sid),
            send_sem=sem, recv_sem=w_recv.at[1 + k, sid], device_id=to, device_id_type=MESH,
        )

    def sent(w, sem):
        pltpu.make_async_remote_copy(
            src_ref=given[w], dst_ref=block(w, 0),
            send_sem=sem, recv_sem=w_recv.at[w, 0], device_id=s_dev, device_id_type=MESH,
        ).wait_send()

    def spread(zz, own=False):
        sid = ident(zz, x, y, c)
        for w in (0, 1):
            send(w, sid, x_dev, x_sem.at[w, 0, zz], own)
            send(w, sid, y_dev, y_sem.at[w, 0, zz], own)
        for w in (0, 1):
            send(w, sid, s_dev, s_sem.at[w, 0, zz], own)

    def side(zz):
        from_x, from_y = ident(zz, xn, y, c), ident(zz, x, yn, c)
        arrive(0, from_x)
        send(0, from_x, y_dev, y_sem.at[0, 1, zz])
        arrive(1, from_y)
        piece_copy(1, from_y, x_dev, x_sem.at[1, 1, zz]).start()
        arrive(1, from_x)
        piece_copy(0, from_x, y_dev, y_sem.at[1, 1, zz]).start()
        arrive(0, from_y)
        for w in (0, 1):
            send(w, from_x, s_dev, s_sem.at[w, 1, zz])
            send(w, from_y, s_dev, s_sem.at[w, 2, zz])

    me = ident(z, x, y, c)

    @pl.when(z < LAYERS - 1)
    def _():
        for w in (0, 1):
            send(w, me, up_dev, z_sem.at[w, 0, z], True)

    @pl.when(z > 0)
    def _():
        for w in (0, 1):
            send(w, me, down_dev, z_sem.at[w, 1, z], True)

    spread(z, True)
    local = [
        pltpu.make_async_copy(wada_ref, ada_buf, loc_sem.at[0]),
        pltpu.make_async_copy(wup_ref, block(0, me), loc_sem.at[1]),
        pltpu.make_async_copy(wdn_ref, block(1, me), loc_sem.at[2]),
    ]
    for copy in local:
        copy.start()

    for t in range(WIN):
        rows = pl.ds(t * part, part)
        whole = state_ref[rows, :]
        high = whole.astype(jnp.bfloat16)
        a_send[t, 0:part, :] = high
        lo_send[t] = (whole - high.astype(jnp.float32)).astype(jnp.bfloat16)
        a_send[t, part : 2 * part, :] = noise_ref[0, rows, :]
        a_send[t, 2 * part : 3 * part, :] = noise_ref[1, rows, :]
    a_recv[tm] = a_send[tm]

    start, adv = start_ref[0], adv_ref[0]
    row = lax.broadcasted_iota(jnp.int32, (2 * WIN, width), 0)
    lane = lax.broadcasted_iota(jnp.int32, (2 * WIN, width), 1)
    half = width // 2
    late = row >= WIN
    steps = (start + jnp.where(late, adv + row - WIN, row)).astype(jnp.float32)
    turn = jnp.where(lane >= half, lane - half, lane).astype(jnp.float32)
    angles = steps * jnp.exp(-math.log(10000.0) * turn / half)
    embed = jnp.where(lane >= half, jnp.sin(angles), jnp.cos(angles))
    condition = jax.nn.silu(embed + cls_ref[...]).astype(jnp.bfloat16)
    for copy in local:
        copy.wait()
    for third in range(3):
        columns = slice(third * width, (third + 1) * width)
        mod[:, columns] = jnp.dot(condition, ada_buf[:, columns], preferred_element_type=jnp.float32)

    first, second = pl.ds(0, 2 * part), pl.ds(2 * part, part)

    def a_copy(d):
        to = (tm + d) % WIN
        return pltpu.make_async_remote_copy(
            src_ref=a_send.at[to, first], dst_ref=a_recv.at[tm, first], send_sem=a_ssem.at[d],
            recv_sem=a_rsem.at[tm], device_id=(to, bt), device_id_type=MESH,
        )

    def n_copy(d):
        to = (tm + d) % WIN
        return pltpu.make_async_remote_copy(
            src_ref=a_send.at[to, second], dst_ref=a_recv.at[tm, second], send_sem=n_ssem.at[d],
            recv_sem=n_rsem.at[tm], device_id=(to, bt), device_id_type=MESH,
        )

    def l_copy(d):
        return pltpu.make_async_remote_copy(
            src_ref=lo_send.at[d], dst_ref=lo_recv, send_sem=l_ssem.at[d],
            recv_sem=l_rsem, device_id=(d, bt), device_id_type=MESH,
        )

    def round_z(r):
        @pl.when(z >= r)
        def _():
            zz = z - r
            sid = ident(zz, x, y, c)
            for w in (0, 1):
                arrive(w, sid)

                @pl.when(z < LAYERS - 1)
                def _():
                    send(w, sid, up_dev, z_sem.at[w, 0, zz])

            spread(zz)

        @pl.when(z + r < LAYERS)
        def _():
            zz = z + r
            sid = ident(zz, x, y, c)
            for w in (0, 1):
                arrive(w, sid)

                @pl.when(z > 0)
                def _():
                    send(w, sid, down_dev, z_sem.at[w, 1, zz])

            spread(zz)

    def round_side(r):
        if r == 0:
            side(z)
            return

        @pl.when(z >= r)
        def _():
            side(z - r)

        @pl.when(z + r < LAYERS)
        def _():
            side(z + r)

    round_z(1)
    round_side(0)
    round_z(2)
    for d in range(1, WIN):
        a_copy(d).start()

    @pl.when(tm == 0)
    def _():
        lo_recv[...] = lo_send[0]
        for d in range(1, WIN):
            l_copy(d).start()

    round_side(1)
    round_z(3)
    round_side(2)
    round_side(3)
    for d in range(1, WIN):
        n_copy(d).start()

    def a_arrive(d):
        src = (tm + d) % WIN
        pltpu.make_async_remote_copy(
            src_ref=a_send.at[src, first], dst_ref=a_recv.at[src, first], send_sem=a_ssem.at[d],
            recv_sem=a_rsem.at[src], device_id=(src, bt), device_id_type=MESH,
        ).wait_recv()

    def n_arrive(d):
        src = (tm + d) % WIN
        pltpu.make_async_remote_copy(
            src_ref=a_send.at[src, second], dst_ref=a_recv.at[src, second], send_sem=n_ssem.at[d],
            recv_sem=n_rsem.at[src], device_id=(src, bt), device_id_type=MESH,
        ).wait_recv()

    for d in range(1, WIN):
        a_arrive(d)

    @pl.when(tm > 0)
    def _():
        l_copy(1).wait_recv()

    for j in range(WIN):
        cur[j] = a_recv[j, 0:part, :].astype(jnp.float32)

    def before_mlp(s):
        @pl.loop(0, WIN)
        def _(j):
            now = cur[j]
            centred = now - jnp.mean(now, axis=1, keepdims=True)
            var = jnp.mean(centred * centred, axis=1, keepdims=True)
            normed = centred * lax.rsqrt(var + EPSILON)
            shift = mod[pl.ds(s * WIN + j, 1), 0:width]
            scale = mod[pl.ds(s * WIN + j, 1), width : 2 * width]
            rows = pl.ds(pl.multiple_of(j * part, part), part)
            hid[rows, :] = (normed * (1.0 + scale) + shift).astype(jnp.bfloat16)
            acc[rows, :] = jnp.zeros((part, width), jnp.float32)

    def activations(first, count):
        rows = pl.ds(pl.multiple_of(first, 128), count)
        before = lax.dot_general(
            up_full[rows, :], hid[...], (((1,), (1,)), ((), ())), preferred_element_type=jnp.float32
        )
        return rows, jax.nn.gelu(before, approximate=True).astype(jnp.bfloat16).T

    def mlp(first, count):
        rows, act = activations(first, count)
        acc[...] += jnp.dot(act, dn_full[rows, :], preferred_element_type=jnp.float32)

    def after_mlp(base):
        pre[0] = base
        for j in range(WIN):
            k = start + j
            rows = pl.ds(j * part, part)
            gate = mod[j : j + 1, 2 * width : 3 * width]
            noise = a_recv[j, part : 2 * part, :].astype(jnp.float32)
            pre[j + 1] = pre[j] + (dt_ref[k] * (gate * acc[rows, :] - cur[j]) + sg_ref[k] * noise)

    before_mlp(0)
    flip = z // 2
    near = z + flip * (3 - 2 * z)

    @pl.loop(0, LAYERS)
    def _(p):
        early = 1 - p // 2
        order = p + near * early * (1 - 2 * p)
        zz = order + flip * (3 - 2 * order)
        across = ident(zz, xn, yn, c)
        arrive(0, across)
        for k in (0, 1):
            piece_copy(k, across, s_dev, s_sem.at[1, 3, zz]).wait_recv()
        for w in (0, 1):
            send(w, across, s_dev, s_sem.at[w, 3, zz])
        for xx in (0, 1):
            for yy in (0, 1):
                for w in (0, 1):
                    arrive(w, ident(zz, xx, yy, cn))

        mlp(zz * layer, layer)

    after_mlp(cur[0] + lo_recv[...].astype(jnp.float32))
    for j in range(WIN):
        cur[j] = pre[jnp.minimum(adv + j, WIN)]
    before_mlp(1)
    rows_used = (WIN - 1) * part

    @pl.loop(0, LAYERS)
    def _(i):
        rows, act = activations(i * layer, layer)
        act_all[:, rows] = act

    own_rows = pl.ds(pl.multiple_of(tm * part, part), part)

    def o_copy(b, d):
        to = (tm + d) % WIN
        return pltpu.make_async_remote_copy(
            src_ref=o_send.at[to, :, spans[b]], dst_ref=out_ref.at[own_rows, spans[b]],
            send_sem=o_ssem.at[b, d], recv_sem=o_rsem.at[b, tm],
            device_id=(to, bt), device_id_type=MESH,
        )

    def o_arrive(b, d):
        src = (tm + d) % WIN
        pltpu.make_async_remote_copy(
            src_ref=o_send.at[src, :, spans[b]],
            dst_ref=out_ref.at[pl.ds(pl.multiple_of(src * part, part), part), spans[b]],
            send_sem=o_ssem.at[b, d], recv_sem=o_rsem.at[b, src],
            device_id=(src, bt), device_id_type=MESH,
        ).wait_recv()

    for d in range(1, WIN):
        n_arrive(d)
    edges = tuple(width * e // 9 for e in SPLIT)
    spans = tuple(pl.ds(lo, hi - lo) for lo, hi in zip(edges, edges[1:]))
    for b, (lo, hi) in enumerate(zip(edges, edges[1:])):
        mlp_out = jnp.dot(act_all[0:rows_used, :], dn_full[:, lo:hi], preferred_element_type=jnp.float32)
        total = cur[0, :, lo:hi]
        for j in range(WIN):
            o_send[j, :, lo:hi] = total.astype(jnp.bfloat16)
            if j == WIN - 1:
                break
            k = start + adv + j
            gate = mod[WIN + j : WIN + j + 1, 2 * width + lo : 2 * width + hi]
            noise = a_recv[j, 2 * part : 3 * part, lo:hi].astype(jnp.float32)
            drift = gate * mlp_out[j * part : (j + 1) * part] - cur[j, :, lo:hi]
            total = total + (dt_ref[k] * drift + sg_ref[k] * noise)
        for d in range(1, WIN):
            o_copy(b, d).start()
    mine = pltpu.make_async_copy(o_send.at[tm], out_ref.at[own_rows], loc_sem.at[0])
    mine.start()

    for zz in range(LAYERS):
        for w in (0, 1):
            @pl.when((z < LAYERS - 1) & (zz <= z))
            def _():
                sent(w, z_sem.at[w, 0, zz])

            @pl.when((z > 0) & (zz >= z))
            def _():
                sent(w, z_sem.at[w, 1, zz])

            sent(w, x_sem.at[w, 0, zz])
            sent(w, y_sem.at[w, 0, zz])
            for kind in range(4):
                sent(w, s_sem.at[w, kind, zz])
        sent(0, y_sem.at[0, 1, zz])
        piece_copy(1, 0, s_dev, x_sem.at[1, 1, zz]).wait_send()
        piece_copy(0, 0, s_dev, y_sem.at[1, 1, zz]).wait_send()
    for d in range(1, WIN):
        a_copy(d).wait_send()
        n_copy(d).wait_send()

    @pl.when(tm == 0)
    def _():
        for d in range(1, WIN):
            l_copy(d).wait_send()

    mine.wait()
    for b in range(len(spans)):
        for d in range(1, WIN):
            o_arrive(b, d)
            o_copy(b, d).wait_send()


def per_device_fused(
    state, noise_draws, class_vec, window_start, advance, step_dt, step_sigma, w_ada, w_up, w_down
):
    tokens, width = state.shape[2:]
    hidden = w_up.shape[0] * WIN * 4
    part = tokens // WIN
    bf16, f32 = jnp.bfloat16, jnp.float32
    vmem, smem = pl.BlockSpec(memory_space=pltpu.VMEM), pl.BlockSpec(memory_space=pltpu.SMEM)
    dma = pltpu.SemaphoreType.DMA
    flops = 2 * 2 * 2 * tokens * width * hidden
    out = pl.pallas_call(
        fused,
        out_shape=jax.ShapeDtypeStruct((tokens, width), bf16),
        in_specs=[smem] * 4 + [vmem] * 5 + [pl.BlockSpec(memory_space=pl.ANY)],
        out_specs=pl.BlockSpec(memory_space=pl.ANY),
        scratch_shapes=[
            pltpu.VMEM((hidden, width), bf16),
            pltpu.VMEM((hidden, width), bf16),
            pltpu.VMEM(w_ada.shape, bf16),
            pltpu.VMEM((2 * WIN, 3 * width), f32),
            pltpu.VMEM((WIN, 3 * part, width), bf16),
            pltpu.VMEM((WIN, 3 * part, width), bf16),
            pltpu.VMEM((WIN, part, width), bf16),
            pltpu.VMEM((part, width), bf16),
            pltpu.VMEM((WIN, part, width), f32),
            pltpu.VMEM((tokens, width), bf16),
            pltpu.VMEM((tokens, width), f32),
            pltpu.VMEM((WIN + 1, part, width), f32),
            pltpu.VMEM((WIN, part, width), bf16),
            pltpu.VMEM((tokens, hidden), bf16),
            dma((3,)),
            dma((3, 32)),
            dma((2, 2, LAYERS)),
            dma((2, 2, LAYERS)),
            dma((2, 2, LAYERS)),
            dma((2, 4, LAYERS)),
            dma((WIN,)),
            dma((WIN,)),
            dma((WIN,)),
            dma((WIN,)),
            dma((WIN,)),
            dma,
            dma((len(SPLIT) - 1, WIN)),
            dma((len(SPLIT) - 1, WIN)),
        ],
        compiler_params=pltpu.CompilerParams(
            collective_id=0, has_side_effects=True, vmem_limit_bytes=58 * 2**20
        ),
        cost_estimate=pl.CostEstimate(flops=flops, bytes_accessed=2 * w_ada.size, transcendentals=0),
        name="picard",
    )(
        window_start, advance, step_dt, step_sigma, class_vec,
        state[0, 0], noise_draws[:, 0, 0], w_up, w_down, w_ada,
    )
    return out.astype(f32)[None, None]


def solution(mesh):
    in_specs = (
        P("tm", "batch", None, None),
        P(None, "tm", "batch", None, None),
        P("batch", None),
        P("batch"),
        P("batch"),
        P(),
        P(),
        P(),
        P(("tm", "batch"), None),
        P(("tm", "batch"), None),
    )
    out_specs = P("tm", "batch", None, None)
    small = mesh.shape["tm"] == WIN and mesh.shape["batch"] == 4
    return jax.shard_map(
        per_device_fused if small else per_device,
        mesh=mesh, in_specs=in_specs, out_specs=out_specs, check_vma=False,
    )
```

```python
import functools
import math

import jax
import jax.numpy as jnp
from jax import lax
from jax.experimental import pallas as pl
from jax.experimental.pallas import tpu as pltpu
from jax.sharding import PartitionSpec as P

SLIDE_BITS = 3
MESH = pl.DeviceIdType.MESH
WIN = 8
LAYERS = 4

EPSILON = 1e-06


def spread_2(shard, axis, root):
    mine = lax.axis_index(axis) == root
    return lax.psum(jnp.where(mine, shard, jnp.zeros_like(shard)), axis)


def carried_in(part, axis, combine, identity):
    place = lax.axis_index(axis)
    gathered = lax.all_gather(part, axis)
    state = jnp.zeros_like(part) + jnp.asarray(identity, part.dtype)

    def one(turn, state):
        return combine(state, lax.dynamic_index_in_dim(gathered, turn, 0, False))

    return lax.fori_loop(0, place, one, state)


def from_behind(shard, axis, by):
    peers = lax.axis_size(axis)
    pairs = [(i, i + by) for i in range(peers) if 0 <= i + by < peers]
    return lax.ppermute(shard, axis, pairs)


def time_embed(steps_now, half_width):
    frequency = jnp.exp(-math.log(10000.0) * jnp.arange(half_width, dtype=jnp.float32) / half_width)
    angles = steps_now.astype(jnp.float32)[:, None] * frequency[None, :]
    return jnp.concatenate([jnp.cos(angles), jnp.sin(angles)], axis=1)


def dense_pair(hidden_rows, up_rows, down_rows):
    before = lax.dot_general(
        hidden_rows, up_rows, (((1,), (1,)), ((), ())), preferred_element_type=jnp.float32
    )
    activated = jax.nn.gelu(before, approximate=True).astype(jnp.bfloat16)
    return jnp.dot(activated, down_rows, preferred_element_type=jnp.float32)


def combine_sum(earlier, later):
    return earlier + later


def increment(current, noise_now, steps_now, class_vec, step_dt, step_sigma, w_ada, mlp_apply):
    images, tokens, channels = current.shape
    step_table = lax.iota(jnp.int32, step_dt.shape[0])
    onehot = (steps_now[:, None] == step_table[None, :]).astype(jnp.float32)
    step_size = jnp.sum(onehot * step_dt[None, :], axis=1)
    spread = jnp.sum(onehot * step_sigma[None, :], axis=1)
    condition = jax.nn.silu(time_embed(steps_now, channels // 2) + class_vec).astype(jnp.bfloat16)
    modulation = jnp.dot(condition, w_ada, preferred_element_type=jnp.float32)
    shift_by = modulation[:, :channels]
    scale_by = modulation[:, channels : 2 * channels]
    gate_by = modulation[:, 2 * channels :]
    mean_val = jnp.mean(current, axis=2, keepdims=True)
    centred = current - mean_val
    var_val = jnp.mean(centred * centred, axis=2, keepdims=True)
    normed = centred * lax.rsqrt(var_val + EPSILON)
    hidden_in = (normed * (1.0 + scale_by[:, None, :]) + shift_by[:, None, :]).astype(jnp.bfloat16)
    mlp_out = mlp_apply(hidden_in.reshape(images * tokens, channels)).reshape(
        images, tokens, channels
    )
    drift = gate_by[:, None, :] * mlp_out - current
    return step_size[:, None, None] * drift + spread[:, None, None] * noise_now.astype(jnp.float32)


def per_device(
    state, noise_draws, class_vec, window_start, advance, step_dt, step_sigma, w_ada, w_up, w_down
):
    window_size = lax.axis_size("tm")
    position = lax.axis_index("tm")
    up_whole, down_whole = (
        lax.all_gather(w_up, ("tm", "batch"), axis=0, tiled=True),
        lax.all_gather(w_down, ("tm", "batch"), axis=0, tiled=True),
    )

    def mlp_apply(hidden_rows):
        return dense_pair(hidden_rows, up_whole, down_whole)

    def sweep(current, noise_now, starts):
        steps_now = starts + position
        step_inc = increment(
            current, noise_now, steps_now, class_vec, step_dt, step_sigma, w_ada, mlp_apply
        )
        base_rows = spread_2(current, "tm", 0)
        prefix = carried_in(step_inc, "tm", combine_sum, jnp.zeros_like(step_inc))
        updated = base_rows + prefix
        return (updated, step_inc)

    updated, step_inc = sweep(state[0], noise_draws[0, 0], window_start)
    end_rows = updated + step_inc
    tail_rows = jnp.where(position == window_size - 1, end_rows, jnp.zeros_like(end_rows))
    moved = updated
    for section_bit in range(SLIDE_BITS):
        distance = 1 << section_bit
        arrived, arrived_tail = from_behind((moved, tail_rows), "tm", -distance)
        taken = advance >> section_bit & 1 == 1
        outside = position + distance >= window_size
        incoming = jnp.where(outside, tail_rows, arrived)
        moved = jnp.where(taken[:, None, None], incoming, moved)
        tail_rows = jnp.where(position >= window_size - distance, tail_rows, arrived_tail)
    final_rows, leftover = sweep(moved, noise_draws[1, 0], window_start + advance)
    return final_rows[None]


SPLIT = (0, 2, 6, 9)
TURNED = 2


def fused(
    start_ref, adv_ref, dt_ref, sg_ref, cls_ref, state_ref, noise_ref, wup_ref, wdn_ref, wada_ref,
    out_ref,
    up_full, dn_full, ada_buf, mod, a_send, a_recv, lo_send, lo_recv, cur, hid, acc, pre, o_send, act_all,
    loc_sem, w_recv, z_sem, x_sem, y_sem, s_sem, a_ssem, a_rsem, n_ssem, n_rsem, l_ssem, l_rsem, o_ssem, o_rsem,
):
    tokens, width = state_ref.shape
    part = tokens // WIN
    depth = wup_ref.shape[0]
    layer = 8 * depth
    tm, bt = lax.axis_index("tm"), lax.axis_index("batch")
    z, x = tm // 2, tm % 2
    y, c = bt // 2, bt % 2
    xn, yn, cn = 1 - x, 1 - y, 1 - c

    def dev(zz, xx, yy, cc):
        return (zz * 2 + xx, yy * 2 + cc)

    x_dev, y_dev, s_dev = dev(z, xn, y, c), dev(z, x, yn, c), dev(z, x, y, cn)
    up_dev, down_dev = dev(z + 1, x, y, c), dev(z - 1, x, y, c)

    barrier = pltpu.get_barrier_semaphore()
    for d in range(1, WIN):
        pl.semaphore_signal(barrier, inc=1, device_id=((tm + d) % WIN, bt), device_id_type=MESH)
    pl.semaphore_signal(barrier, inc=1, device_id=y_dev, device_id_type=MESH)
    pl.semaphore_signal(barrier, inc=1, device_id=s_dev, device_id_type=MESH)
    pl.semaphore_wait(barrier, WIN + 1)

    full = (up_full, dn_full)
    given = (wup_ref, wdn_ref)

    def block(w, sid):
        return full[w].at[pl.ds(pl.multiple_of(sid * depth, 16), depth)]

    def ident(zz, xx, yy, cc):
        return (zz * 2 + xx) * 4 + yy * 2 + cc

    def send(w, sid, to, sem, own=False):
        pltpu.make_async_remote_copy(
            src_ref=given[w] if own else block(w, sid), dst_ref=block(w, sid),
            send_sem=sem, recv_sem=w_recv.at[w, sid], device_id=to, device_id_type=MESH,
        ).start()

    def arrive(w, sid):
        pltpu.make_async_remote_copy(
            src_ref=block(w, sid), dst_ref=block(w, sid),
            send_sem=s_sem.at[w, 0, 0], recv_sem=w_recv.at[w, sid], device_id=s_dev, device_id_type=MESH,
        ).wait_recv()

    turned = depth * TURNED // 9 // 16 * 16
    cuts = ((0, turned), (turned, depth - turned))

    def piece(k, sid):
        return dn_full.at[pl.ds(pl.multiple_of(sid * depth + cuts[k][0], 16), cuts[k][1])]

    def piece_copy(k, sid, to, sem):
        return pltpu.make_async_remote_copy(
            src_ref=piece(k, sid), dst_ref=piece(k, sid),
            send_sem=sem, recv_sem=w_recv.at[1 + k, sid], device_id=to, device_id_type=MESH,
        )

    def sent(w, sem):
        pltpu.make_async_remote_copy(
            src_ref=given[w], dst_ref=block(w, 0),
            send_sem=sem, recv_sem=w_recv.at[w, 0], device_id=s_dev, device_id_type=MESH,
        ).wait_send()

    def spread(zz, own=False):
        sid = ident(zz, x, y, c)
        for w in (0, 1):
            send(w, sid, x_dev, x_sem.at[w, 0, zz], own)
            send(w, sid, y_dev, y_sem.at[w, 0, zz], own)
        for w in (0, 1):
            send(w, sid, s_dev, s_sem.at[w, 0, zz], own)

    def side(zz):
        from_x, from_y = ident(zz, xn, y, c), ident(zz, x, yn, c)
        arrive(0, from_x)
        send(0, from_x, y_dev, y_sem.at[0, 1, zz])
        arrive(1, from_y)
        piece_copy(1, from_y, x_dev, x_sem.at[1, 1, zz]).start()
        arrive(1, from_x)
        piece_copy(0, from_x, y_dev, y_sem.at[1, 1, zz]).start()
        arrive(0, from_y)
        for w in (0, 1):
            send(w, from_x, s_dev, s_sem.at[w, 1, zz])
            send(w, from_y, s_dev, s_sem.at[w, 2, zz])

    me = ident(z, x, y, c)

    @pl.when(z < LAYERS - 1)
    def _():
        for w in (0, 1):
            send(w, me, up_dev, z_sem.at[w, 0, z], True)

    @pl.when(z > 0)
    def _():
        for w in (0, 1):
            send(w, me, down_dev, z_sem.at[w, 1, z], True)

    spread(z, True)
    local = [
        pltpu.make_async_copy(wada_ref, ada_buf, loc_sem.at[0]),
        pltpu.make_async_copy(wup_ref, block(0, me), loc_sem.at[1]),
        pltpu.make_async_copy(wdn_ref, block(1, me), loc_sem.at[2]),
    ]
    for copy in local:
        copy.start()

    for t in range(WIN):
        rows = pl.ds(t * part, part)
        whole = state_ref[rows, :]
        high = whole.astype(jnp.bfloat16)
        a_send[t, 0:part, :] = high
        lo_send[t] = (whole - high.astype(jnp.float32)).astype(jnp.bfloat16)
        a_send[t, part : 2 * part, :] = noise_ref[0, rows, :]
        a_send[t, 2 * part : 3 * part, :] = noise_ref[1, rows, :]
    a_recv[tm] = a_send[tm]

    start, adv = start_ref[0], adv_ref[0]
    row = lax.broadcasted_iota(jnp.int32, (2 * WIN, width), 0)
    lane = lax.broadcasted_iota(jnp.int32, (2 * WIN, width), 1)
    half = width // 2
    late = row >= WIN
    steps = (start + jnp.where(late, adv + row - WIN, row)).astype(jnp.float32)
    turn = jnp.where(lane >= half, lane - half, lane).astype(jnp.float32)
    angles = steps * jnp.exp(-math.log(10000.0) * turn / half)
    embed = jnp.where(lane >= half, jnp.sin(angles), jnp.cos(angles))
    condition = jax.nn.silu(embed + cls_ref[...]).astype(jnp.bfloat16)
    for copy in local:
        copy.wait()
    for third in range(3):
        columns = slice(third * width, (third + 1) * width)
        mod[:, columns] = jnp.dot(condition, ada_buf[:, columns], preferred_element_type=jnp.float32)

    first, second = pl.ds(0, 2 * part), pl.ds(2 * part, part)

    def a_copy(d):
        to = (tm + d) % WIN
        return pltpu.make_async_remote_copy(
            src_ref=a_send.at[to, first], dst_ref=a_recv.at[tm, first], send_sem=a_ssem.at[d],
            recv_sem=a_rsem.at[tm], device_id=(to, bt), device_id_type=MESH,
        )

    def n_copy(d):
        to = (tm + d) % WIN
        return pltpu.make_async_remote_copy(
            src_ref=a_send.at[to, second], dst_ref=a_recv.at[tm, second], send_sem=n_ssem.at[d],
            recv_sem=n_rsem.at[tm], device_id=(to, bt), device_id_type=MESH,
        )

    def l_copy(d):
        return pltpu.make_async_remote_copy(
            src_ref=lo_send.at[d], dst_ref=lo_recv, send_sem=l_ssem.at[d],
            recv_sem=l_rsem, device_id=(d, bt), device_id_type=MESH,
        )

    def round_z(r):
        @pl.when(z >= r)
        def _():
            zz = z - r
            sid = ident(zz, x, y, c)
            for w in (0, 1):
                arrive(w, sid)

                @pl.when(z < LAYERS - 1)
                def _():
                    send(w, sid, up_dev, z_sem.at[w, 0, zz])

            spread(zz)

        @pl.when(z + r < LAYERS)
        def _():
            zz = z + r
            sid = ident(zz, x, y, c)
            for w in (0, 1):
                arrive(w, sid)

                @pl.when(z > 0)
                def _():
                    send(w, sid, down_dev, z_sem.at[w, 1, zz])

            spread(zz)

    def round_side(r):
        if r == 0:
            side(z)
            return

        @pl.when(z >= r)
        def _():
            side(z - r)

        @pl.when(z + r < LAYERS)
        def _():
            side(z + r)

    round_z(1)
    round_side(0)
    round_z(2)
    for d in range(1, WIN):
        a_copy(d).start()

    @pl.when(tm == 0)
    def _():
        lo_recv[...] = lo_send[0]
        for d in range(1, WIN):
            l_copy(d).start()

    round_side(1)
    round_z(3)
    round_side(2)

    def a_arrive(d):
        src = (tm + d) % WIN
        pltpu.make_async_remote_copy(
            src_ref=a_send.at[src, first], dst_ref=a_recv.at[src, first], send_sem=a_ssem.at[d],
            recv_sem=a_rsem.at[src], device_id=(src, bt), device_id_type=MESH,
        ).wait_recv()

    def n_arrive(d):
        src = (tm + d) % WIN
        pltpu.make_async_remote_copy(
            src_ref=a_send.at[src, second], dst_ref=a_recv.at[src, second], send_sem=n_ssem.at[d],
            recv_sem=n_rsem.at[src], device_id=(src, bt), device_id_type=MESH,
        ).wait_recv()

    for d in range(1, WIN):
        a_arrive(d)

    @pl.when(tm > 0)
    def _():
        l_copy(1).wait_recv()

    for j in range(WIN):
        cur[j] = a_recv[j, 0:part, :].astype(jnp.float32)

    def before_mlp(s):
        @pl.loop(0, WIN)
        def _(j):
            now = cur[j]
            centred = now - jnp.mean(now, axis=1, keepdims=True)
            var = jnp.mean(centred * centred, axis=1, keepdims=True)
            normed = centred * lax.rsqrt(var + EPSILON)
            shift = mod[pl.ds(s * WIN + j, 1), 0:width]
            scale = mod[pl.ds(s * WIN + j, 1), width : 2 * width]
            rows = pl.ds(pl.multiple_of(j * part, part), part)
            hid[rows, :] = (normed * (1.0 + scale) + shift).astype(jnp.bfloat16)
            acc[rows, :] = jnp.zeros((part, width), jnp.float32)

    def mlp(first, count):
        rows = pl.ds(pl.multiple_of(first, 128), count)
        before = lax.dot_general(
            hid[...], up_full[rows, :], (((1,), (1,)), ((), ())), preferred_element_type=jnp.float32
        )
        act = jax.nn.gelu(before, approximate=True).astype(jnp.bfloat16)
        acc[...] += jnp.dot(act, dn_full[rows, :], preferred_element_type=jnp.float32)

    def after_mlp(base):
        pre[0] = base
        for j in range(WIN):
            k = start + j
            rows = pl.ds(j * part, part)
            gate = mod[j : j + 1, 2 * width : 3 * width]
            noise = a_recv[j, part : 2 * part, :].astype(jnp.float32)
            pre[j + 1] = pre[j] + (dt_ref[k] * (gate * acc[rows, :] - cur[j]) + sg_ref[k] * noise)

    before_mlp(0)
    flip = z // 2
    near = z + flip * (3 - 2 * z)

    def through(p):
        early = 1 - p // 2
        order = p + near * early * (1 - 2 * p)
        zz = order + flip * (3 - 2 * order)
        across = ident(zz, xn, yn, c)
        arrive(0, across)
        for k in (0, 1):
            piece_copy(k, across, s_dev, s_sem.at[1, 3, zz]).wait_recv()
        for w in (0, 1):
            send(w, across, s_dev, s_sem.at[w, 3, zz])
        for xx in (0, 1):
            for yy in (0, 1):
                for w in (0, 1):
                    arrive(w, ident(zz, xx, yy, cn))

        @pl.loop(0, 3)
        def _(i):
            mlp(zz * layer + i * (layer // 3), layer // 3)

    pl.loop(0, 2)(through)
    round_side(3)
    for d in range(1, WIN):
        n_copy(d).start()
    pl.loop(2, LAYERS)(through)
    after_mlp(cur[0] + lo_recv[...].astype(jnp.float32))
    for j in range(WIN):
        cur[j] = pre[jnp.minimum(adv + j, WIN)]
    before_mlp(1)
    rows_used = (WIN - 1) * part
    hidden = LAYERS * layer

    @pl.loop(0, 3)
    def _(i):
        for k in range(3):
            rows = pl.ds(pl.multiple_of((i * 3 + k) * (hidden // 9), 128), hidden // 9)
            before = lax.dot_general(
                hid[0:rows_used, :], up_full[rows, :], (((1,), (1,)), ((), ())),
                preferred_element_type=jnp.float32,
            )
            act_all[:, rows] = jax.nn.gelu(before, approximate=True).astype(jnp.bfloat16)

    own_rows = pl.ds(pl.multiple_of(tm * part, part), part)

    def o_copy(b, d):
        to = (tm + d) % WIN
        return pltpu.make_async_remote_copy(
            src_ref=o_send.at[to, :, spans[b]], dst_ref=out_ref.at[own_rows, spans[b]],
            send_sem=o_ssem.at[b, d], recv_sem=o_rsem.at[b, tm],
            device_id=(to, bt), device_id_type=MESH,
        )

    def o_arrive(b, d):
        src = (tm + d) % WIN
        pltpu.make_async_remote_copy(
            src_ref=o_send.at[src, :, spans[b]],
            dst_ref=out_ref.at[pl.ds(pl.multiple_of(src * part, part), part), spans[b]],
            send_sem=o_ssem.at[b, d], recv_sem=o_rsem.at[b, src],
            device_id=(src, bt), device_id_type=MESH,
        ).wait_recv()

    for d in range(1, WIN):
        n_arrive(d)
    edges = tuple(width * e // 9 for e in SPLIT)
    spans = tuple(pl.ds(lo, hi - lo) for lo, hi in zip(edges, edges[1:]))
    for b, (lo, hi) in enumerate(zip(edges, edges[1:])):
        mlp_out = jnp.dot(act_all[...], dn_full[:, lo:hi], preferred_element_type=jnp.float32)
        total = cur[0, :, lo:hi]
        for j in range(WIN):
            o_send[j, :, lo:hi] = total.astype(jnp.bfloat16)
            if j == WIN - 1:
                break
            k = start + adv + j
            gate = mod[WIN + j : WIN + j + 1, 2 * width + lo : 2 * width + hi]
            noise = a_recv[j, 2 * part : 3 * part, lo:hi].astype(jnp.float32)
            drift = gate * mlp_out[j * part : (j + 1) * part] - cur[j, :, lo:hi]
            total = total + (dt_ref[k] * drift + sg_ref[k] * noise)
        for d in range(1, WIN):
            o_copy(b, d).start()
    mine = pltpu.make_async_copy(o_send.at[tm], out_ref.at[own_rows], loc_sem.at[0])
    mine.start()

    for zz in range(LAYERS):
        for w in (0, 1):
            @pl.when((z < LAYERS - 1) & (zz <= z))
            def _():
                sent(w, z_sem.at[w, 0, zz])

            @pl.when((z > 0) & (zz >= z))
            def _():
                sent(w, z_sem.at[w, 1, zz])

            sent(w, x_sem.at[w, 0, zz])
            sent(w, y_sem.at[w, 0, zz])
            for kind in range(4):
                sent(w, s_sem.at[w, kind, zz])
        sent(0, y_sem.at[0, 1, zz])
        piece_copy(1, 0, s_dev, x_sem.at[1, 1, zz]).wait_send()
        piece_copy(0, 0, s_dev, y_sem.at[1, 1, zz]).wait_send()
    for d in range(1, WIN):
        a_copy(d).wait_send()
        n_copy(d).wait_send()

    @pl.when(tm == 0)
    def _():
        for d in range(1, WIN):
            l_copy(d).wait_send()

    mine.wait()
    for b in range(len(spans)):
        for d in range(1, WIN):
            o_arrive(b, d)
            o_copy(b, d).wait_send()


def per_device_fused(
    state, noise_draws, class_vec, window_start, advance, step_dt, step_sigma, w_ada, w_up, w_down
):
    tokens, width = state.shape[2:]
    hidden = w_up.shape[0] * WIN * 4
    part = tokens // WIN
    bf16, f32 = jnp.bfloat16, jnp.float32
    vmem, smem = pl.BlockSpec(memory_space=pltpu.VMEM), pl.BlockSpec(memory_space=pltpu.SMEM)
    dma = pltpu.SemaphoreType.DMA
    flops = 2 * 2 * 2 * tokens * width * hidden
    out = pl.pallas_call(
        fused,
        out_shape=jax.ShapeDtypeStruct((tokens, width), bf16),
        in_specs=[smem] * 4 + [vmem] * 5 + [pl.BlockSpec(memory_space=pl.ANY)],
        out_specs=pl.BlockSpec(memory_space=pl.ANY),
        scratch_shapes=[
            pltpu.VMEM((hidden, width), bf16),
            pltpu.VMEM((hidden, width), bf16),
            pltpu.VMEM(w_ada.shape, bf16),
            pltpu.VMEM((2 * WIN, 3 * width), f32),
            pltpu.VMEM((WIN, 3 * part, width), bf16),
            pltpu.VMEM((WIN, 3 * part, width), bf16),
            pltpu.VMEM((WIN, part, width), bf16),
            pltpu.VMEM((part, width), bf16),
            pltpu.VMEM((WIN, part, width), f32),
            pltpu.VMEM((tokens, width), bf16),
            pltpu.VMEM((tokens, width), f32),
            pltpu.VMEM((WIN + 1, part, width), f32),
            pltpu.VMEM((WIN, part, width), bf16),
            pltpu.VMEM(((WIN - 1) * part, hidden), bf16),
            dma((3,)),
            dma((3, 32)),
            dma((2, 2, LAYERS)),
            dma((2, 2, LAYERS)),
            dma((2, 2, LAYERS)),
            dma((2, 4, LAYERS)),
            dma((WIN,)),
            dma((WIN,)),
            dma((WIN,)),
            dma((WIN,)),
            dma((WIN,)),
            dma,
            dma((len(SPLIT) - 1, WIN)),
            dma((len(SPLIT) - 1, WIN)),
        ],
        compiler_params=pltpu.CompilerParams(
            collective_id=0, has_side_effects=True, vmem_limit_bytes=58 * 2**20
        ),
        cost_estimate=pl.CostEstimate(flops=flops, bytes_accessed=2 * w_ada.size, transcendentals=0),
        name="picard",
    )(
        window_start, advance, step_dt, step_sigma, class_vec,
        state[0, 0], noise_draws[:, 0, 0], w_up, w_down, w_ada,
    )
    return out.astype(f32)[None, None]


def solution(mesh):
    in_specs = (
        P("tm", "batch", None, None),
        P(None, "tm", "batch", None, None),
        P("batch", None),
        P("batch"),
        P("batch"),
        P(),
        P(),
        P(),
        P(("tm", "batch"), None),
        P(("tm", "batch"), None),
    )
    out_specs = P("tm", "batch", None, None)
    small = mesh.shape["tm"] == WIN and mesh.shape["batch"] == 4
    return jax.shard_map(
        per_device_fused if small else per_device,
        mesh=mesh, in_specs=in_specs, out_specs=out_specs, check_vma=False,
    )
```

```python
import functools
import math

import jax
import jax.numpy as jnp
from jax import lax
from jax.experimental import pallas as pl
from jax.experimental.pallas import tpu as pltpu
from jax.sharding import PartitionSpec as P

SLIDE_BITS = 3
MESH = pl.DeviceIdType.MESH
WIN = 8
LAYERS = 4

EPSILON = 1e-06


def spread_2(shard, axis, root):
    mine = lax.axis_index(axis) == root
    return lax.psum(jnp.where(mine, shard, jnp.zeros_like(shard)), axis)


def carried_in(part, axis, combine, identity):
    place = lax.axis_index(axis)
    gathered = lax.all_gather(part, axis)
    state = jnp.zeros_like(part) + jnp.asarray(identity, part.dtype)

    def one(turn, state):
        return combine(state, lax.dynamic_index_in_dim(gathered, turn, 0, False))

    return lax.fori_loop(0, place, one, state)


def from_behind(shard, axis, by):
    peers = lax.axis_size(axis)
    pairs = [(i, i + by) for i in range(peers) if 0 <= i + by < peers]
    return lax.ppermute(shard, axis, pairs)


def time_embed(steps_now, half_width):
    frequency = jnp.exp(-math.log(10000.0) * jnp.arange(half_width, dtype=jnp.float32) / half_width)
    angles = steps_now.astype(jnp.float32)[:, None] * frequency[None, :]
    return jnp.concatenate([jnp.cos(angles), jnp.sin(angles)], axis=1)


def dense_pair(hidden_rows, up_rows, down_rows):
    before = lax.dot_general(
        hidden_rows, up_rows, (((1,), (1,)), ((), ())), preferred_element_type=jnp.float32
    )
    activated = jax.nn.gelu(before, approximate=True).astype(jnp.bfloat16)
    return jnp.dot(activated, down_rows, preferred_element_type=jnp.float32)


def combine_sum(earlier, later):
    return earlier + later


def increment(current, noise_now, steps_now, class_vec, step_dt, step_sigma, w_ada, mlp_apply):
    images, tokens, channels = current.shape
    step_table = lax.iota(jnp.int32, step_dt.shape[0])
    onehot = (steps_now[:, None] == step_table[None, :]).astype(jnp.float32)
    step_size = jnp.sum(onehot * step_dt[None, :], axis=1)
    spread = jnp.sum(onehot * step_sigma[None, :], axis=1)
    condition = jax.nn.silu(time_embed(steps_now, channels // 2) + class_vec).astype(jnp.bfloat16)
    modulation = jnp.dot(condition, w_ada, preferred_element_type=jnp.float32)
    shift_by = modulation[:, :channels]
    scale_by = modulation[:, channels : 2 * channels]
    gate_by = modulation[:, 2 * channels :]
    mean_val = jnp.mean(current, axis=2, keepdims=True)
    centred = current - mean_val
    var_val = jnp.mean(centred * centred, axis=2, keepdims=True)
    normed = centred * lax.rsqrt(var_val + EPSILON)
    hidden_in = (normed * (1.0 + scale_by[:, None, :]) + shift_by[:, None, :]).astype(jnp.bfloat16)
    mlp_out = mlp_apply(hidden_in.reshape(images * tokens, channels)).reshape(
        images, tokens, channels
    )
    drift = gate_by[:, None, :] * mlp_out - current
    return step_size[:, None, None] * drift + spread[:, None, None] * noise_now.astype(jnp.float32)


def per_device(
    state, noise_draws, class_vec, window_start, advance, step_dt, step_sigma, w_ada, w_up, w_down
):
    window_size = lax.axis_size("tm")
    position = lax.axis_index("tm")
    up_whole, down_whole = (
        lax.all_gather(w_up, ("tm", "batch"), axis=0, tiled=True),
        lax.all_gather(w_down, ("tm", "batch"), axis=0, tiled=True),
    )

    def mlp_apply(hidden_rows):
        return dense_pair(hidden_rows, up_whole, down_whole)

    def sweep(current, noise_now, starts):
        steps_now = starts + position
        step_inc = increment(
            current, noise_now, steps_now, class_vec, step_dt, step_sigma, w_ada, mlp_apply
        )
        base_rows = spread_2(current, "tm", 0)
        prefix = carried_in(step_inc, "tm", combine_sum, jnp.zeros_like(step_inc))
        updated = base_rows + prefix
        return (updated, step_inc)

    updated, step_inc = sweep(state[0], noise_draws[0, 0], window_start)
    end_rows = updated + step_inc
    tail_rows = jnp.where(position == window_size - 1, end_rows, jnp.zeros_like(end_rows))
    moved = updated
    for section_bit in range(SLIDE_BITS):
        distance = 1 << section_bit
        arrived, arrived_tail = from_behind((moved, tail_rows), "tm", -distance)
        taken = advance >> section_bit & 1 == 1
        outside = position + distance >= window_size
        incoming = jnp.where(outside, tail_rows, arrived)
        moved = jnp.where(taken[:, None, None], incoming, moved)
        tail_rows = jnp.where(position >= window_size - distance, tail_rows, arrived_tail)
    final_rows, leftover = sweep(moved, noise_draws[1, 0], window_start + advance)
    return final_rows[None]


SPLIT = (0, 2, 6, 9)
TURNED = 2


def fused(
    start_ref, adv_ref, dt_ref, sg_ref, cls_ref, state_ref, noise_ref, wup_ref, wdn_ref, wada_ref,
    out_ref,
    up_full, dn_full, ada_buf, mod, a_send, a_recv, lo_send, lo_recv, cur, hid, acc, pre, o_send, act_all,
    loc_sem, w_recv, z_sem, x_sem, y_sem, s_sem, a_ssem, a_rsem, n_ssem, n_rsem, l_ssem, l_rsem, o_ssem, o_rsem,
):
    tokens, width = state_ref.shape
    part = tokens // WIN
    depth = wup_ref.shape[0]
    layer = 8 * depth
    tm, bt = lax.axis_index("tm"), lax.axis_index("batch")
    z, x = tm // 2, tm % 2
    y, c = bt // 2, bt % 2
    xn, yn, cn = 1 - x, 1 - y, 1 - c

    def dev(zz, xx, yy, cc):
        return (zz * 2 + xx, yy * 2 + cc)

    x_dev, y_dev, s_dev = dev(z, xn, y, c), dev(z, x, yn, c), dev(z, x, y, cn)
    up_dev, down_dev = dev(z + 1, x, y, c), dev(z - 1, x, y, c)

    barrier = pltpu.get_barrier_semaphore()
    for d in range(1, WIN):
        pl.semaphore_signal(barrier, inc=1, device_id=((tm + d) % WIN, bt), device_id_type=MESH)
    pl.semaphore_signal(barrier, inc=1, device_id=y_dev, device_id_type=MESH)
    pl.semaphore_signal(barrier, inc=1, device_id=s_dev, device_id_type=MESH)
    pl.semaphore_wait(barrier, WIN + 1)

    full = (up_full, dn_full)
    given = (wup_ref, wdn_ref)

    def block(w, sid):
        return full[w].at[pl.ds(pl.multiple_of(sid * depth, 16), depth)]

    def ident(zz, xx, yy, cc):
        return (zz * 2 + xx) * 4 + yy * 2 + cc

    def send(w, sid, to, sem, own=False):
        pltpu.make_async_remote_copy(
            src_ref=given[w] if own else block(w, sid), dst_ref=block(w, sid),
            send_sem=sem, recv_sem=w_recv.at[w, sid], device_id=to, device_id_type=MESH,
        ).start()

    def arrive(w, sid):
        pltpu.make_async_remote_copy(
            src_ref=block(w, sid), dst_ref=block(w, sid),
            send_sem=s_sem.at[w, 0, 0], recv_sem=w_recv.at[w, sid], device_id=s_dev, device_id_type=MESH,
        ).wait_recv()

    turned = depth * TURNED // 9 // 16 * 16
    cuts = ((0, turned), (turned, depth - turned))

    def piece(k, sid):
        return dn_full.at[pl.ds(pl.multiple_of(sid * depth + cuts[k][0], 16), cuts[k][1])]

    def piece_copy(k, sid, to, sem):
        return pltpu.make_async_remote_copy(
            src_ref=piece(k, sid), dst_ref=piece(k, sid),
            send_sem=sem, recv_sem=w_recv.at[1 + k, sid], device_id=to, device_id_type=MESH,
        )

    def sent(w, sem):
        pltpu.make_async_remote_copy(
            src_ref=given[w], dst_ref=block(w, 0),
            send_sem=sem, recv_sem=w_recv.at[w, 0], device_id=s_dev, device_id_type=MESH,
        ).wait_send()

    def spread(zz, own=False):
        sid = ident(zz, x, y, c)
        for w in (0, 1):
            send(w, sid, x_dev, x_sem.at[w, 0, zz], own)
            send(w, sid, y_dev, y_sem.at[w, 0, zz], own)
        for w in (0, 1):
            send(w, sid, s_dev, s_sem.at[w, 0, zz], own)

    def side(zz):
        from_x, from_y = ident(zz, xn, y, c), ident(zz, x, yn, c)
        arrive(0, from_x)
        send(0, from_x, y_dev, y_sem.at[0, 1, zz])
        arrive(1, from_y)
        piece_copy(1, from_y, x_dev, x_sem.at[1, 1, zz]).start()
        arrive(1, from_x)
        piece_copy(0, from_x, y_dev, y_sem.at[1, 1, zz]).start()
        arrive(0, from_y)
        for w in (0, 1):
            send(w, from_x, s_dev, s_sem.at[w, 1, zz])
            send(w, from_y, s_dev, s_sem.at[w, 2, zz])

    me = ident(z, x, y, c)

    @pl.when(z < LAYERS - 1)
    def _():
        for w in (0, 1):
            send(w, me, up_dev, z_sem.at[w, 0, z], True)

    @pl.when(z > 0)
    def _():
        for w in (0, 1):
            send(w, me, down_dev, z_sem.at[w, 1, z], True)

    spread(z, True)
    local = [
        pltpu.make_async_copy(wada_ref, ada_buf, loc_sem.at[0]),
        pltpu.make_async_copy(wup_ref, block(0, me), loc_sem.at[1]),
        pltpu.make_async_copy(wdn_ref, block(1, me), loc_sem.at[2]),
    ]
    for copy in local:
        copy.start()

    for t in range(WIN):
        rows = pl.ds(t * part, part)
        whole = state_ref[rows, :]
        high = whole.astype(jnp.bfloat16)
        a_send[t, 0:part, :] = high
        lo_send[t] = (whole - high.astype(jnp.float32)).astype(jnp.bfloat16)
        a_send[t, part : 2 * part, :] = noise_ref[0, rows, :]
        a_send[t, 2 * part : 3 * part, :] = noise_ref[1, rows, :]
    a_recv[tm] = a_send[tm]

    start, adv = start_ref[0], adv_ref[0]
    row = lax.broadcasted_iota(jnp.int32, (2 * WIN, width), 0)
    lane = lax.broadcasted_iota(jnp.int32, (2 * WIN, width), 1)
    half = width // 2
    late = row >= WIN
    steps = (start + jnp.where(late, adv + row - WIN, row)).astype(jnp.float32)
    turn = jnp.where(lane >= half, lane - half, lane).astype(jnp.float32)
    angles = steps * jnp.exp(-math.log(10000.0) * turn / half)
    embed = jnp.where(lane >= half, jnp.sin(angles), jnp.cos(angles))
    condition = jax.nn.silu(embed + cls_ref[...]).astype(jnp.bfloat16)
    for copy in local:
        copy.wait()
    for third in range(3):
        columns = slice(third * width, (third + 1) * width)
        mod[:, columns] = jnp.dot(condition, ada_buf[:, columns], preferred_element_type=jnp.float32)

    first, spans_n = pl.ds(0, part), (pl.ds(part, part), pl.ds(2 * part, part))

    def a_copy(d):
        to = (tm + d) % WIN
        return pltpu.make_async_remote_copy(
            src_ref=a_send.at[to, first], dst_ref=a_recv.at[tm, first], send_sem=a_ssem.at[d],
            recv_sem=a_rsem.at[tm], device_id=(to, bt), device_id_type=MESH,
        )

    def n_copy(s, d):
        to = (tm + d) % WIN
        return pltpu.make_async_remote_copy(
            src_ref=a_send.at[to, spans_n[s]], dst_ref=a_recv.at[tm, spans_n[s]], send_sem=n_ssem.at[s, d],
            recv_sem=n_rsem.at[s, tm], device_id=(to, bt), device_id_type=MESH,
        )

    def l_copy(d):
        return pltpu.make_async_remote_copy(
            src_ref=lo_send.at[d], dst_ref=lo_recv, send_sem=l_ssem.at[d],
            recv_sem=l_rsem, device_id=(d, bt), device_id_type=MESH,
        )

    def round_z(r):
        @pl.when(z >= r)
        def _():
            zz = z - r
            sid = ident(zz, x, y, c)
            for w in (0, 1):
                arrive(w, sid)

                @pl.when(z < LAYERS - 1)
                def _():
                    send(w, sid, up_dev, z_sem.at[w, 0, zz])

            spread(zz)

        @pl.when(z + r < LAYERS)
        def _():
            zz = z + r
            sid = ident(zz, x, y, c)
            for w in (0, 1):
                arrive(w, sid)

                @pl.when(z > 0)
                def _():
                    send(w, sid, down_dev, z_sem.at[w, 1, zz])

            spread(zz)

    def round_side(r):
        if r == 0:
            side(z)
            return

        @pl.when(z >= r)
        def _():
            side(z - r)

        @pl.when(z + r < LAYERS)
        def _():
            side(z + r)

    round_z(1)
    round_side(0)
    round_z(2)
    for d in range(1, WIN):
        a_copy(d).start()

    @pl.when(tm == 0)
    def _():
        lo_recv[...] = lo_send[0]
        for d in range(1, WIN):
            l_copy(d).start()

    round_side(1)
    round_z(3)
    round_side(2)

    def a_arrive(d):
        src = (tm + d) % WIN
        pltpu.make_async_remote_copy(
            src_ref=a_send.at[src, first], dst_ref=a_recv.at[src, first], send_sem=a_ssem.at[d],
            recv_sem=a_rsem.at[src], device_id=(src, bt), device_id_type=MESH,
        ).wait_recv()

    def n_arrive(s, d):
        src = (tm + d) % WIN
        pltpu.make_async_remote_copy(
            src_ref=a_send.at[src, spans_n[s]], dst_ref=a_recv.at[src, spans_n[s]], send_sem=n_ssem.at[s, d],
            recv_sem=n_rsem.at[s, src], device_id=(src, bt), device_id_type=MESH,
        ).wait_recv()

    for d in range(1, WIN):
        n_copy(0, d).start()
    for d in range(1, WIN):
        a_arrive(d)

    @pl.when(tm > 0)
    def _():
        l_copy(1).wait_recv()

    for j in range(WIN):
        cur[j] = a_recv[j, 0:part, :].astype(jnp.float32)

    def before_mlp(s):
        @pl.loop(0, WIN)
        def _(j):
            now = cur[j]
            centred = now - jnp.mean(now, axis=1, keepdims=True)
            var = jnp.mean(centred * centred, axis=1, keepdims=True)
            normed = centred * lax.rsqrt(var + EPSILON)
            shift = mod[pl.ds(s * WIN + j, 1), 0:width]
            scale = mod[pl.ds(s * WIN + j, 1), width : 2 * width]
            rows = pl.ds(pl.multiple_of(j * part, part), part)
            hid[rows, :] = (normed * (1.0 + scale) + shift).astype(jnp.bfloat16)
            acc[rows, :] = jnp.zeros((part, width), jnp.float32)

    def mlp(first, count):
        rows = pl.ds(pl.multiple_of(first, 128), count)
        before = lax.dot_general(
            hid[...], up_full[rows, :], (((1,), (1,)), ((), ())), preferred_element_type=jnp.float32
        )
        act = jax.nn.gelu(before, approximate=True).astype(jnp.bfloat16)
        acc[...] += jnp.dot(act, dn_full[rows, :], preferred_element_type=jnp.float32)

    def after_mlp(base):
        pre[0] = base
        for j in range(WIN):
            k = start + j
            rows = pl.ds(j * part, part)
            gate = mod[j : j + 1, 2 * width : 3 * width]
            noise = a_recv[j, part : 2 * part, :].astype(jnp.float32)
            pre[j + 1] = pre[j] + (dt_ref[k] * (gate * acc[rows, :] - cur[j]) + sg_ref[k] * noise)

    before_mlp(0)
    flip = z // 2
    near = z + flip * (3 - 2 * z)

    def through(p):
        early = 1 - p // 2
        order = p + near * early * (1 - 2 * p)
        zz = order + flip * (3 - 2 * order)
        across = ident(zz, xn, yn, c)
        arrive(0, across)
        for k in (0, 1):
            piece_copy(k, across, s_dev, s_sem.at[1, 3, zz]).wait_recv()
        for w in (0, 1):
            send(w, across, s_dev, s_sem.at[w, 3, zz])
        for xx in (0, 1):
            for yy in (0, 1):
                for w in (0, 1):
                    arrive(w, ident(zz, xx, yy, cn))

        @pl.loop(0, 3)
        def _(i):
            mlp(zz * layer + i * (layer // 3), layer // 3)

    pl.loop(0, 2)(through)
    round_side(3)
    for d in range(1, WIN):
        n_copy(1, d).start()
    pl.loop(2, LAYERS)(through)
    for d in range(1, WIN):
        n_arrive(0, d)
    after_mlp(cur[0] + lo_recv[...].astype(jnp.float32))
    for j in range(WIN):
        cur[j] = pre[jnp.minimum(adv + j, WIN)]
    before_mlp(1)
    rows_used = (WIN - 1) * part
    hidden = LAYERS * layer

    @pl.loop(0, 3)
    def _(i):
        for k in range(3):
            rows = pl.ds(pl.multiple_of((i * 3 + k) * (hidden // 9), 128), hidden // 9)
            before = lax.dot_general(
                hid[0:rows_used, :], up_full[rows, :], (((1,), (1,)), ((), ())),
                preferred_element_type=jnp.float32,
            )
            act_all[:, rows] = jax.nn.gelu(before, approximate=True).astype(jnp.bfloat16)

    own_rows = pl.ds(pl.multiple_of(tm * part, part), part)

    def o_copy(b, d):
        to = (tm + d) % WIN
        return pltpu.make_async_remote_copy(
            src_ref=o_send.at[to, :, spans[b]], dst_ref=out_ref.at[own_rows, spans[b]],
            send_sem=o_ssem.at[b, d], recv_sem=o_rsem.at[b, tm],
            device_id=(to, bt), device_id_type=MESH,
        )

    def o_arrive(b, d):
        src = (tm + d) % WIN
        pltpu.make_async_remote_copy(
            src_ref=o_send.at[src, :, spans[b]],
            dst_ref=out_ref.at[pl.ds(pl.multiple_of(src * part, part), part), spans[b]],
            send_sem=o_ssem.at[b, d], recv_sem=o_rsem.at[b, src],
            device_id=(src, bt), device_id_type=MESH,
        ).wait_recv()

    for d in range(1, WIN):
        n_arrive(1, d)
    edges = tuple(width * e // 9 for e in SPLIT)
    spans = tuple(pl.ds(lo, hi - lo) for lo, hi in zip(edges, edges[1:]))
    for b, (lo, hi) in enumerate(zip(edges, edges[1:])):
        mlp_out = jnp.dot(act_all[...], dn_full[:, lo:hi], preferred_element_type=jnp.float32)
        total = cur[0, :, lo:hi]
        for j in range(WIN):
            o_send[j, :, lo:hi] = total.astype(jnp.bfloat16)
            if j == WIN - 1:
                break
            k = start + adv + j
            gate = mod[WIN + j : WIN + j + 1, 2 * width + lo : 2 * width + hi]
            noise = a_recv[j, 2 * part : 3 * part, lo:hi].astype(jnp.float32)
            drift = gate * mlp_out[j * part : (j + 1) * part] - cur[j, :, lo:hi]
            total = total + (dt_ref[k] * drift + sg_ref[k] * noise)
        for d in range(1, WIN):
            o_copy(b, d).start()
    mine = pltpu.make_async_copy(o_send.at[tm], out_ref.at[own_rows], loc_sem.at[0])
    mine.start()

    for zz in range(LAYERS):
        for w in (0, 1):
            @pl.when((z < LAYERS - 1) & (zz <= z))
            def _():
                sent(w, z_sem.at[w, 0, zz])

            @pl.when((z > 0) & (zz >= z))
            def _():
                sent(w, z_sem.at[w, 1, zz])

            sent(w, x_sem.at[w, 0, zz])
            sent(w, y_sem.at[w, 0, zz])
            for kind in range(4):
                sent(w, s_sem.at[w, kind, zz])
        sent(0, y_sem.at[0, 1, zz])
        piece_copy(1, 0, s_dev, x_sem.at[1, 1, zz]).wait_send()
        piece_copy(0, 0, s_dev, y_sem.at[1, 1, zz]).wait_send()
    for d in range(1, WIN):
        a_copy(d).wait_send()
        n_copy(0, d).wait_send()
        n_copy(1, d).wait_send()

    @pl.when(tm == 0)
    def _():
        for d in range(1, WIN):
            l_copy(d).wait_send()

    mine.wait()
    for b in range(len(spans)):
        for d in range(1, WIN):
            o_arrive(b, d)
            o_copy(b, d).wait_send()


def per_device_fused(
    state, noise_draws, class_vec, window_start, advance, step_dt, step_sigma, w_ada, w_up, w_down
):
    tokens, width = state.shape[2:]
    hidden = w_up.shape[0] * WIN * 4
    part = tokens // WIN
    bf16, f32 = jnp.bfloat16, jnp.float32
    vmem, smem = pl.BlockSpec(memory_space=pltpu.VMEM), pl.BlockSpec(memory_space=pltpu.SMEM)
    dma = pltpu.SemaphoreType.DMA
    flops = 2 * 2 * 2 * tokens * width * hidden
    out = pl.pallas_call(
        fused,
        out_shape=jax.ShapeDtypeStruct((tokens, width), bf16),
        in_specs=[smem] * 4 + [vmem] * 5 + [pl.BlockSpec(memory_space=pl.ANY)],
        out_specs=pl.BlockSpec(memory_space=pl.ANY),
        scratch_shapes=[
            pltpu.VMEM((hidden, width), bf16),
            pltpu.VMEM((hidden, width), bf16),
            pltpu.VMEM(w_ada.shape, bf16),
            pltpu.VMEM((2 * WIN, 3 * width), f32),
            pltpu.VMEM((WIN, 3 * part, width), bf16),
            pltpu.VMEM((WIN, 3 * part, width), bf16),
            pltpu.VMEM((WIN, part, width), bf16),
            pltpu.VMEM((part, width), bf16),
            pltpu.VMEM((WIN, part, width), f32),
            pltpu.VMEM((tokens, width), bf16),
            pltpu.VMEM((tokens, width), f32),
            pltpu.VMEM((WIN + 1, part, width), f32),
            pltpu.VMEM((WIN, part, width), bf16),
            pltpu.VMEM(((WIN - 1) * part, hidden), bf16),
            dma((3,)),
            dma((3, 32)),
            dma((2, 2, LAYERS)),
            dma((2, 2, LAYERS)),
            dma((2, 2, LAYERS)),
            dma((2, 4, LAYERS)),
            dma((WIN,)),
            dma((WIN,)),
            dma((2, WIN)),
            dma((2, WIN)),
            dma((WIN,)),
            dma,
            dma((len(SPLIT) - 1, WIN)),
            dma((len(SPLIT) - 1, WIN)),
        ],
        compiler_params=pltpu.CompilerParams(
            collective_id=0, has_side_effects=True, vmem_limit_bytes=58 * 2**20
        ),
        cost_estimate=pl.CostEstimate(flops=flops, bytes_accessed=2 * w_ada.size, transcendentals=0),
        name="picard",
    )(
        window_start, advance, step_dt, step_sigma, class_vec,
        state[0, 0], noise_draws[:, 0, 0], w_up, w_down, w_ada,
    )
    return out.astype(f32)[None, None]


def solution(mesh):
    in_specs = (
        P("tm", "batch", None, None),
        P(None, "tm", "batch", None, None),
        P("batch", None),
        P("batch"),
        P("batch"),
        P(),
        P(),
        P(),
        P(("tm", "batch"), None),
        P(("tm", "batch"), None),
    )
    out_specs = P("tm", "batch", None, None)
    small = mesh.shape["tm"] == WIN and mesh.shape["batch"] == 4
    return jax.shard_map(
        per_device_fused if small else per_device,
        mesh=mesh, in_specs=in_specs, out_specs=out_specs, check_vma=False,
    )
```
